32 devices in a mesh: space: 8 (over z, x), vel: 4 (over y, core).
Axes of the slice: x: 2, y: 2, z: 4, core: 2. Of those that a mesh axis runs over, the one named last changes fastest.
Arguments:
- dist: bfloat16 [128, 64, 4096], P('space', None, 'vel'), may hold values from -6 to 6
- send_faces: int32 [8, 2, 16], P('space'), may hold values from 0 to 95
- send_count: int32 [8, 2], P('space'), may hold values from 1 to 16, as said below
- source_face: int32 [128, 6], P('space'), may hold values from 0 to 127, as said below
- subface: int32 [128, 6], P('space'), may hold values from 0 to 4
- alpha: float32 [4, 4096], replicated, may hold values from -1 to 1
- beta: float32 [5, 4096], replicated, may hold values from -1 to 1
Outputs:
- relaxed: bfloat16 [128, 64, 4096], P('space', None, 'vel')
The draws below stay inside these ranges and needn't reach their ends.
Inputs may be any that keep to these rules, and one draw needn't show every extreme that they name: `source_face`: for each face of a block: below 96 a local face of the same block; from 96 the 16 slots of the previous block's block toward the next one, then the 16 slots of the next block's block toward the previous one. Every slot of these two blocks is read by exactly one face of the block. `send_count`: for each direction some block's padded trace block is full. `send_faces`: local face numbers, element times 6 plus face.
All inputs are finite; a program needn't handle non-finite values.
Results may differ from the reference program's by a relative error of at most 0.0057.
Values may be sent and summed in bfloat16 or wider, within the bound.
A program may use at most 64 MiB of HBM per device.

```python
import jax
import jax.numpy as jnp
import numpy as np
from jax import lax

E_DEV = 16
NODES = 64
VSIDE = 16
MODES = 4
ELEMS = 128
VEL = 4096
MAXB = 16
N_SPACE = 8


def draw_source_face(key, part):
    faces = 6 * E_DEV
    blocks = ELEMS // E_DEV

    def one_block(block_key):
        order = jax.random.permutation(block_key, faces)
        local = jax.random.randint(jax.random.fold_in(block_key, 1), (faces,), 0, faces)
        remote = faces + jnp.arange(2 * MAXB)
        return local.at[order[:2 * MAXB]].set(remote).reshape(E_DEV, 6)
    keys = jax.random.split(jax.random.fold_in(key, 11), blocks)
    return jax.vmap(one_block)(keys).reshape(ELEMS, 6).astype(jnp.int32)


def draw_send_count(key, part):
    blocks = ELEMS // E_DEV
    counts = jax.random.randint(jax.random.fold_in(key, 23), (blocks, 2), 1, MAXB + 1)
    chosen = jax.random.randint(jax.random.fold_in(key, 29), (2,), 0, blocks)
    return counts.at[chosen, jnp.arange(2)].set(MAXB).astype(jnp.int32)


def touch_ends(values, stream_key, least, largest):
    shape = values.shape
    spot = [jax.random.randint(jax.random.fold_in(stream_key, axis), (), 0, shape[axis]) for axis in range(len(shape))]
    values = values.at[tuple(spot)].set(least)
    longest = shape.index(max(shape))
    spot[longest] = (spot[longest] + 1) % shape[longest]
    return values.at[tuple(spot)].set(largest)


def shard_levels(key, shape, cuts, low, largest):
    level, own = 1.0, jax.random.fold_in(key, 6)
    for position, parts in cuts:
        heights = jnp.exp(jax.random.uniform(jax.random.fold_in(own, position), (parts,), jnp.float32, low / len(cuts), largest / len(cuts)))
        level = level * jnp.repeat(heights, shape[position] // parts).reshape([-1 if axis == position else 1 for axis in range(len(shape))])
    return level


def centred(key, dims, width, most, pieces=(), kind=jnp.bfloat16):
    loudness = shard_levels(key, dims, pieces, -0.22, 0.18) if pieces else 1.0
    entries = jax.random.normal(key, dims, jnp.float32) * width * loudness
    return jnp.minimum(jnp.maximum(entries, -most), most).astype(kind)


def setup_inputs(seed: int = 0) -> dict:
    seeds = jax.random.split(jax.random.key(seed), 8)
    return {
        "dist": centred(seeds[0], (ELEMS, NODES, VEL), 1.0, 6.0, ((0, 8), (2, 4))),
        "send_faces": touch_ends(jax.random.randint(seeds[1], (N_SPACE, 2, MAXB), 0, 6 * E_DEV), jax.random.fold_in(seeds[1], 1), 0, (6 * E_DEV) - 1).astype(jnp.int32),
        "send_count": draw_send_count(jax.random.fold_in(seeds[7], 71), 0),
        "source_face": draw_source_face(jax.random.fold_in(seeds[7], 71), 0),
        "subface": touch_ends(jax.random.randint(seeds[4], (ELEMS, 6), 0, 5), jax.random.fold_in(seeds[4], 1), 0, 4).astype(jnp.int32),
        "alpha": jnp.clip(jax.random.uniform(seeds[5], (MODES, VEL), jnp.float32, -1.0, 1.0), -1.0, 1.0),
        "beta": jnp.clip(jax.random.uniform(seeds[6], (MODES + 1, VEL), jnp.float32, -1.0, 1.0), -1.0, 1.0),
    }


courant = 0.1
lift_weight = 6.0
relax_step = 0.5
highest = lax.Precision.HIGHEST

def lobatto_points():
    return np.array([-1.0, -1.0 / np.sqrt(5.0), 1.0 / np.sqrt(5.0), 1.0])

def lagrange_table(targets):
    points = lobatto_points()
    result = np.ones((targets.shape[0], 4))
    for column in range(4):
        for second in range(4):
            if second != column:
                result[:, column] = result[:, column] * (targets - points[second]) / (points[column] - points[second])
    return result

def derivative_table():
    points = lobatto_points()
    result = np.zeros((4, 4))
    for row_at in range(4):
        for column in range(4):
            total = 0.0
            for skipped in range(4):
                if skipped != column:
                    factor = 1.0 / (points[column] - points[skipped])
                    for second in range(4):
                        if second != column and second != skipped:
                            factor = factor * (points[row_at] - points[second]) / (points[column] - points[second])
                    total = total + factor
            result[row_at, column] = total
    return result

def cosine_table():
    index_list = np.arange(VSIDE)
    result = np.sqrt(2.0 / VSIDE) * np.cos(np.pi * (index_list[None, :] + 0.5) * index_list[:, None] / VSIDE)
    result[0] = result[0] / np.sqrt(2.0)
    return result

def static_tables():
    derivative = derivative_table()
    eye_four = np.eye(4)
    gradients = np.stack([np.kron(np.kron(derivative, eye_four), eye_four), np.kron(np.kron(eye_four, derivative), eye_four), np.kron(np.kron(eye_four, eye_four), derivative)])
    selector = np.zeros((96, 64))
    for axis_at in range(3):
        for side_at in range(2):
            filled = 0
            for node_at in range(64):
                digits = (node_at // 16, node_at // 4 % 4, node_at % 4)
                if digits[axis_at] == 3 * side_at:
                    selector[(2 * axis_at + side_at) * 16 + filled, node_at] = 1.0
                    filled = filled + 1
    points = lobatto_points()
    halves = [lagrange_table((points - 1.0) / 2.0), lagrange_table((points + 1.0) / 2.0)]
    mortar = np.stack([np.eye(16)] + [np.kron(halves[(which - 1) // 2], halves[(which - 1) % 2]) for which in range(1, 5)])
    return (gradients, selector, mortar)

def velocity_components(first, count):
    index_list = first + jnp.arange(count)
    along = [index_list // (VSIDE * VSIDE), index_list // VSIDE % VSIDE, index_list % VSIDE]
    return jnp.stack([(entry.astype(jnp.float32) + 0.5) * (2.0 / VSIDE) - 1.0 for entry in along])

def outgoing_blocks(block, sends, counts, selector):
    faces = jnp.einsum('tn,env->etv', selector, block.astype(jnp.float32)).astype(jnp.bfloat16)
    rows = faces.reshape(E_DEV * 6, 16, VEL)
    picked = rows[sends.reshape(-1)].reshape(2, MAXB, 16, VEL)
    live = jnp.arange(MAXB)[None, :] < counts[:, None]
    return jnp.where(live[:, :, None, None], picked, jnp.zeros_like(picked))

def transport(block, from_prev, from_next, sources, levels, tables, speeds):
    gradients, selector, mortar = tables
    values = block.astype(jnp.float32)
    rows = jnp.einsum('tn,env->etv', selector, values).astype(jnp.bfloat16).reshape(E_DEV * 6, 16, VEL)
    drift = jnp.zeros_like(values)
    for axis_at in range(3):
        drift = drift + speeds[axis_at] * jnp.einsum('nm,emv->env', gradients[axis_at], values)
    table = jnp.concatenate([rows, from_prev, from_next], axis=0)
    neighbour = table[sources.reshape(-1)].astype(jnp.float32)
    projected = jnp.einsum('ftu,fuv->ftv', mortar[levels.reshape(-1)], neighbour)
    inflow = jnp.minimum(jnp.stack([-speeds[0], speeds[0], -speeds[1], speeds[1], -speeds[2], speeds[2]]), 0.0)
    jump = (rows.astype(jnp.float32) - projected).reshape(E_DEV, 6, 16, VEL) * inflow[None, :, None, :]
    lifted = jnp.einsum('tn,etv->env', selector, jump.reshape(E_DEV, 96, VEL), precision=highest)
    return (values - courant * drift + courant * lift_weight * lifted).astype(jnp.bfloat16)

def collide_element(element, kernels, cosine):
    values = element.astype(jnp.float32)
    cube = values.reshape(NODES, VSIDE, VSIDE, VSIDE)
    spectrum = jnp.einsum('ai,nijk->najk', cosine, cube, precision=highest)
    spectrum = jnp.einsum('bj,najk->nabk', cosine, spectrum, precision=highest)
    spectrum = jnp.einsum('ck,nabk->nabc', cosine, spectrum, precision=highest)
    filtered = spectrum[:, None] * kernels[None]
    fields = jnp.einsum('ai,nmabc->nmibc', cosine, filtered, precision=highest)
    fields = jnp.einsum('bj,nmibc->nmijc', cosine, fields, precision=highest)
    fields = jnp.einsum('ck,nmijc->nmijk', cosine, fields, precision=highest).reshape(NODES, 2 * MODES + 1, VEL)
    gain = lax.optimization_barrier(jnp.sum(fields[:, :MODES] * fields[:, MODES:2 * MODES], axis=1))
    loss = values * fields[:, 2 * MODES]
    return (values + relax_step * (gain - loss)).astype(jnp.bfloat16)

def reference(dist, send_faces, send_count, source_face, subface, alpha, beta):
    gradients, selector, mortar = static_tables()
    tables = (jnp.asarray(gradients, jnp.bfloat16).astype(jnp.float32), jnp.asarray(selector, jnp.float32), jnp.asarray(mortar, jnp.bfloat16).astype(jnp.float32))
    speeds = velocity_components(0, VEL)
    blocks = dist.reshape(N_SPACE, E_DEV, NODES, VEL)

    def send_step(item):
        return outgoing_blocks(item[0], item[1], item[2], tables[1])
    outgoing = lax.map(send_step, (blocks, send_faces, send_count))
    from_prev = jnp.roll(outgoing[:, 1], 1, axis=0)
    from_next = jnp.roll(outgoing[:, 0], -1, axis=0)

    def move_step(item):
        return transport(item[0], item[1], item[2], item[3], item[4], tables, speeds)
    updated = lax.map(move_step, (blocks, from_prev, from_next, source_face.reshape(N_SPACE, E_DEV, 6), subface.reshape(N_SPACE, E_DEV, 6)))
    cosine = jnp.asarray(cosine_table(), jnp.float32)
    kernels = jnp.concatenate([alpha, beta], axis=0).reshape(2 * MODES + 1, VSIDE, VSIDE, VSIDE)

    def collide_step(element):
        return collide_element(element, kernels, cosine)
    return lax.map(collide_step, updated.reshape(ELEMS, NODES, VEL))
```

```python
import jax
import jax.numpy as jnp
import numpy as np
from jax import lax
from jax.experimental import pallas as pl
from jax.experimental.pallas import tpu as pltpu
from jax.sharding import PartitionSpec as P

VSIDE = 16
VEL = 4096


courant = 0.1
lift_weight = 6.0
relax_step = 0.5


def passed_along(block, axis, distance):
    devices = range(lax.axis_size(axis))
    route = [((i - distance) % len(devices), i) for i in devices]
    return lax.ppermute(block, axis, route)


def lobatto_points():
    return np.array([-1.0, -1.0 / np.sqrt(5.0), 1.0 / np.sqrt(5.0), 1.0])


def lagrange_table(targets):
    points = lobatto_points()
    result = np.ones((targets.shape[0], 4))
    for column in range(4):
        for second in range(4):
            if second != column:
                result[:, column] = (
                    result[:, column]
                    * (targets - points[second])
                    / (points[column] - points[second])
                )
    return result


def derivative_table():
    points = lobatto_points()
    result = np.zeros((4, 4))
    for row_at in range(4):
        for column in range(4):
            total = 0.0
            for skipped in range(4):
                if skipped != column:
                    factor = 1.0 / (points[column] - points[skipped])
                    for second in range(4):
                        if second != column and second != skipped:
                            factor = (
                                factor
                                * (points[row_at] - points[second])
                                / (points[column] - points[second])
                            )
                    total = total + factor
            result[row_at, column] = total
    return result


def cosine_table():
    index_list = np.arange(VSIDE)
    result = np.sqrt(2.0 / VSIDE) * np.cos(
        np.pi * (index_list[None, :] + 0.5) * index_list[:, None] / VSIDE
    )
    result[0] = result[0] / np.sqrt(2.0)
    return result


def static_tables():
    derivative = derivative_table()
    eye_four = np.eye(4)
    gradients = np.stack(
        [
            np.kron(np.kron(derivative, eye_four), eye_four),
            np.kron(np.kron(eye_four, derivative), eye_four),
            np.kron(np.kron(eye_four, eye_four), derivative),
        ]
    )
    selector = np.zeros((96, 64))
    for axis_at in range(3):
        for side_at in range(2):
            filled = 0
            for node_at in range(64):
                digits = (node_at // 16, node_at // 4 % 4, node_at % 4)
                if digits[axis_at] == 3 * side_at:
                    selector[(2 * axis_at + side_at) * 16 + filled, node_at] = 1.0
                    filled = filled + 1
    points = lobatto_points()
    halves = [lagrange_table((points - 1.0) / 2.0), lagrange_table((points + 1.0) / 2.0)]
    mortar = np.stack(
        [np.eye(16)]
        + [np.kron(halves[(which - 1) // 2], halves[(which - 1) % 2]) for which in range(1, 5)]
    )
    return (gradients, selector, mortar)


def velocity_components(first, count):
    index_list = first + jnp.arange(count)
    along = [index_list // (VSIDE * VSIDE), index_list // VSIDE % VSIDE, index_list % VSIDE]
    return jnp.stack([(entry.astype(jnp.float32) + 0.5) * (2.0 / VSIDE) - 1.0 for entry in along])


def face_parts():
    gradients, selector, mortar = static_tables()
    low = jnp.bfloat16
    grad = np.asarray(gradients.reshape(192, 64).astype(low), np.float64)
    mort = np.asarray(mortar.astype(low), np.float64)
    levels = mort.shape[0]
    spread = np.zeros((levels, 192, 96))
    for face in range(6):
        sel = selector[16 * face : 16 * face + 16]
        for level in range(levels):
            spread[level, 64 * (face // 2) : 64 * (face // 2) + 64, 16 * face : 16 * face + 16] = (
                sel.T @ mort[level]
            )
    stacked = np.concatenate(
        [np.broadcast_to(grad, (levels, 192, 64)), 4.0 * spread, 2.0 * spread], axis=2
    )
    return stacked, selector


def trace_kernel(send_ref, count_ref, select_ref, dist_ref, table_ref, out_ref):
    elements = dist_ref.shape[0]
    slots = out_ref.shape[1]

    def fill(e, carry):
        got = jnp.dot(select_ref[...], dist_ref[e], preferred_element_type=jnp.float32)
        table_ref[pl.ds(6 * e, 6)] = got.astype(jnp.bfloat16).reshape(6, 16, got.shape[1])
        return carry

    lax.fori_loop(0, elements, fill, 0)

    def pick(k, carry):
        j = k // slots
        m = k % slots
        got = table_ref[send_ref[j, m]]
        live = (m < count_ref[j]).astype(jnp.bfloat16)
        out_ref[j, m] = got * live
        return carry

    lax.fori_loop(0, 2 * slots, pick, 0)


def transport_kernel(
    source_ref, dist_ref, table_ref, prev_ref, next_ref, w_ref, coef_ref, scale_ref, mask_ref,
    out_ref, full, block,
):
    elements = dist_ref.shape[0]
    local = table_ref.shape[0]
    slots = prev_ref.shape[0]
    full[0:local] = table_ref[...]
    full[local : local + slots] = prev_ref[...]
    full[local + slots : local + 2 * slots] = next_ref[...]

    def step(e, carry):
        here = dist_ref[e]
        block[0:64] = here
        for face in range(6):
            got = full[source_ref[e, face]] * mask_ref[face : face + 1, :]
            block[64 + 16 * face : 80 + 16 * face] = got
            block[160 + 16 * face : 176 + 16 * face] = got
        moved = jnp.dot(w_ref[e], block[...], preferred_element_type=jnp.float32)
        total = coef_ref[...] * here.astype(jnp.float32)
        for axis_at in range(3):
            total = total + scale_ref[axis_at : axis_at + 1, :] * moved[64 * axis_at : 64 * axis_at + 64]
        out_ref[e] = total.astype(jnp.bfloat16)
        return carry

    lax.fori_loop(0, elements, step, 0)


def collide_block(values, kernels, pair_t, pair, outer, outer_t):
    low = jnp.bfloat16
    inner = jnp.dot(values, pair_t, preferred_element_type=jnp.float32).astype(low)
    spectrum = jnp.dot(outer, inner, preferred_element_type=jnp.float32).reshape(16, 16, 256)
    rows = kernels.shape[0]
    modes = (rows - 1) // 2

    def field(m):
        scaled = (spectrum * kernels[m][:, None, :]).astype(low).reshape(256, 256)
        back = jnp.dot(scaled, pair, preferred_element_type=jnp.float32).astype(low)
        return jnp.dot(outer_t, back, preferred_element_type=jnp.float32)

    wide = values.astype(jnp.float32)
    total = -wide * field(2 * modes)
    for m in range(modes):
        total = total + field(m) * field(modes + m)
    return (wide + relax_step * total).astype(low)


def collide_kernel(x_ref, kernel_ref, pair_t_ref, pair_ref, outer_ref, outer_t_ref, out_ref):
    sources = x_ref.shape[0]
    per = x_ref.shape[3] // 256
    parts = [
        x_ref[s, 0, :, 256 * q : 256 * q + 256] for s in range(sources) for q in range(per)
    ]
    values = jnp.concatenate(parts, axis=0)
    got = collide_block(
        values, kernel_ref, pair_t_ref[...], pair_ref[...], outer_ref[...], outer_t_ref[...]
    )
    for s in range(sources):
        for q in range(per):
            at = 16 * (per * s + q)
            out_ref[s, 0, :, 256 * q : 256 * q + 256] = got[at : at + 16]


def on_device(dist, send_faces, send_count, source_face, subface, alpha, beta):
    low = jnp.bfloat16
    elements = dist.shape[0]
    vel_local = dist.shape[2]
    slots = send_faces.shape[2]
    ranks = lax.axis_size("vel")
    smem = pl.BlockSpec(memory_space=pltpu.SMEM)
    vmem = pl.BlockSpec(memory_space=pltpu.VMEM)
    stacked, selector = face_parts()
    params = pltpu.CompilerParams(vmem_limit_bytes=48 * 1024 * 1024)

    table, outgoing = pl.pallas_call(
        trace_kernel,
        out_shape=(
            jax.ShapeDtypeStruct((elements * 6, 16, vel_local), low),
            jax.ShapeDtypeStruct((2, slots, 16, vel_local), low),
        ),
        in_specs=[smem, smem, vmem, vmem],
        out_specs=(vmem, vmem),
        compiler_params=params,
    )(send_faces[0], send_count[0], jnp.asarray(selector, low), dist)
    from_prev = passed_along(outgoing[1], "space", 1)
    from_next = passed_along(outgoing[0], "space", -1)

    speeds = velocity_components(lax.axis_index("vel") * vel_local, vel_local)
    column_level = jnp.concatenate(
        [jnp.zeros((elements, 64), subface.dtype)] + [jnp.repeat(subface, 16, axis=1)] * 2, axis=1
    )
    weights = jnp.zeros((elements, 192, 256), low)
    for level in range(stacked.shape[0]):
        weights = jnp.where(
            column_level[:, None, :] == level, jnp.asarray(stacked[level], low)[None], weights
        )
    digits = np.stack([np.arange(64) // 16, np.arange(64) // 4 % 4, np.arange(64) % 4])
    first = jnp.asarray(digits == 0, jnp.float32)[:, :, None]
    last = jnp.asarray(digits == 3, jnp.float32)[:, :, None]
    up = jnp.maximum(speeds, 0.0)[:, None, :]
    down = jnp.minimum(speeds, 0.0)[:, None, :]
    coef = 1.0 + courant * lift_weight * jnp.sum(last * down - first * up, axis=0)
    mask = jnp.stack(
        [-(speeds > 0).astype(low), (speeds < 0).astype(low)], axis=1
    ).reshape(6, vel_local)
    scale = -courant * speeds

    updated = pl.pallas_call(
        transport_kernel,
        out_shape=jax.ShapeDtypeStruct(dist.shape, low),
        in_specs=[smem] + [vmem] * 8,
        out_specs=vmem,
        scratch_shapes=[
            pltpu.VMEM((elements * 6 + 2 * slots, 16, vel_local), low),
            pltpu.VMEM((256, vel_local), low),
        ],
        compiler_params=params,
    )(source_face, dist, table, from_prev, from_next, weights, coef, scale, mask)

    cosine = cosine_table()
    pair = np.kron(cosine, cosine)
    outer = np.kron(cosine, np.eye(16))
    tables = [jnp.asarray(t, low) for t in (pair.T, pair, outer, outer.T)]
    kernels = jnp.concatenate([alpha, beta], axis=0)
    kernels = kernels.reshape(kernels.shape[0], VSIDE, VSIDE * VSIDE)

    share = elements // ranks
    gathered = lax.all_to_all(
        updated.reshape(ranks, share, 64, vel_local), "vel", split_axis=0, concat_axis=0
    )
    blockspec = pl.BlockSpec((ranks, 1, 16, vel_local), lambda e, g: (0, e, g, 0))
    mixed = pl.pallas_call(
        collide_kernel,
        grid=(share, 4),
        out_shape=jax.ShapeDtypeStruct(gathered.shape, low),
        in_specs=[blockspec] + [vmem] * 5,
        out_specs=blockspec,
        compiler_params=params,
    )(gathered, kernels, *tables)
    relaxed = lax.all_to_all(mixed, "vel", split_axis=0, concat_axis=0)
    return relaxed.reshape(dist.shape)


def solution(mesh):
    return jax.shard_map(
        on_device,
        mesh=mesh,
        in_specs=(
            P("space", None, "vel"),
            P("space", None, None),
            P("space", None),
            P("space", None),
            P("space", None),
            P(),
            P(),
        ),
        out_specs=P("space", None, "vel"),
        check_vma=False,
    )
```

```python
import functools

import jax
import jax.numpy as jnp
import numpy as np
from jax import lax
from jax.experimental import pallas as pl
from jax.experimental.pallas import tpu as pltpu
from jax.sharding import PartitionSpec as P

VSIDE = 16
VEL = 4096


courant = 0.1
lift_weight = 6.0
relax_step = 0.5
MESH = pl.DeviceIdType.MESH


def lobatto_points():
    return np.array([-1.0, -1.0 / np.sqrt(5.0), 1.0 / np.sqrt(5.0), 1.0])


def lagrange_table(targets):
    points = lobatto_points()
    result = np.ones((targets.shape[0], 4))
    for column in range(4):
        for second in range(4):
            if second != column:
                result[:, column] = (
                    result[:, column]
                    * (targets - points[second])
                    / (points[column] - points[second])
                )
    return result


def derivative_table():
    points = lobatto_points()
    result = np.zeros((4, 4))
    for row_at in range(4):
        for column in range(4):
            total = 0.0
            for skipped in range(4):
                if skipped != column:
                    factor = 1.0 / (points[column] - points[skipped])
                    for second in range(4):
                        if second != column and second != skipped:
                            factor = (
                                factor
                                * (points[row_at] - points[second])
                                / (points[column] - points[second])
                            )
                    total = total + factor
            result[row_at, column] = total
    return result


def cosine_table():
    index_list = np.arange(VSIDE)
    result = np.sqrt(2.0 / VSIDE) * np.cos(
        np.pi * (index_list[None, :] + 0.5) * index_list[:, None] / VSIDE
    )
    result[0] = result[0] / np.sqrt(2.0)
    return result


def static_tables():
    derivative = derivative_table()
    eye_four = np.eye(4)
    gradients = np.stack(
        [
            np.kron(np.kron(derivative, eye_four), eye_four),
            np.kron(np.kron(eye_four, derivative), eye_four),
            np.kron(np.kron(eye_four, eye_four), derivative),
        ]
    )
    selector = np.zeros((96, 64))
    for axis_at in range(3):
        for side_at in range(2):
            filled = 0
            for node_at in range(64):
                digits = (node_at // 16, node_at // 4 % 4, node_at % 4)
                if digits[axis_at] == 3 * side_at:
                    selector[(2 * axis_at + side_at) * 16 + filled, node_at] = 1.0
                    filled = filled + 1
    points = lobatto_points()
    halves = [lagrange_table((points - 1.0) / 2.0), lagrange_table((points + 1.0) / 2.0)]
    mortar = np.stack(
        [np.eye(16)]
        + [np.kron(halves[(which - 1) // 2], halves[(which - 1) % 2]) for which in range(1, 5)]
    )
    return (gradients, selector, mortar)


def velocity_components(first, count):
    index_list = first + jnp.arange(count)
    along = [index_list // (VSIDE * VSIDE), index_list // VSIDE % VSIDE, index_list % VSIDE]
    return jnp.stack([(entry.astype(jnp.float32) + 0.5) * (2.0 / VSIDE) - 1.0 for entry in along])


def face_parts():
    gradients, selector, mortar = static_tables()
    low = jnp.bfloat16
    grad = np.asarray(gradients.reshape(192, 64).astype(low), np.float64)
    mort = np.asarray(mortar.astype(low), np.float64)
    levels = mort.shape[0]
    spread = np.zeros((levels, 192, 96))
    for face in range(6):
        sel = selector[16 * face : 16 * face + 16]
        for level in range(levels):
            spread[level, 64 * (face // 2) : 64 * (face // 2) + 64, 16 * face : 16 * face + 16] = (
                sel.T @ mort[level]
            )
    stacked = np.concatenate(
        [np.broadcast_to(grad, (levels, 192, 64)), 4.0 * spread, 2.0 * spread], axis=2
    )
    return stacked, selector


def collide_block(values, kernels, pair_t, pair, outer, outer_t):
    low = jnp.bfloat16
    inner = jnp.dot(values, pair_t, preferred_element_type=jnp.float32).astype(low)
    spectrum = jnp.dot(outer, inner, preferred_element_type=jnp.float32).reshape(16, 16, 256)
    rows = kernels.shape[0]
    modes = (rows - 1) // 2

    def field(m):
        scaled = (spectrum * kernels[m][:, None, :]).astype(low).reshape(256, 256)
        back = jnp.dot(scaled, pair, preferred_element_type=jnp.float32).astype(low)
        return jnp.dot(outer_t, back, preferred_element_type=jnp.float32)

    wide = values.astype(jnp.float32)
    total = -wide * field(2 * modes)
    for m in range(modes):
        total = total + field(m) * field(modes + m)
    return (wide + relax_step * total).astype(low)


def fused_kernel(
    sizes, send_ref, count_ref, source_ref, dist_ref, select_ref, w_ref, coef_ref, scale_ref,
    mask_ref, kernel_ref, pair_t_ref, pair_ref, outer_ref, outer_t_ref, out_ref, *scratch,
):
    chunks, ranks, blocks, slots = sizes
    tables, halo_out, halo_in, moved_out = (
        scratch[chunks * k : chunks * k + chunks] for k in range(4)
    )
    block, gathered, mixed = scratch[4 * chunks : 4 * chunks + 3]
    hs, hr, us, ur, ms, mr, own_sem = scratch[4 * chunks + 3 :]
    elements = dist_ref.shape[0]
    share = elements // ranks
    local = 6 * elements
    low = jnp.bfloat16
    place = lax.axis_index("space")
    me = lax.axis_index("vel")
    after = lax.rem(place + 1, blocks)
    before = lax.rem(place + blocks - 1, blocks)
    peers = [lax.rem(me + k, ranks) for k in range(1, ranks)]

    barrier = pltpu.get_barrier_semaphore()
    for other in (before, after):
        pl.semaphore_signal(barrier, inc=1, device_id={"space": other}, device_id_type=MESH)
    for peer in peers:
        pl.semaphore_signal(barrier, inc=1, device_id={"vel": peer}, device_id_type=MESH)

    def send(src, dst, send_sem, recv_sem, target):
        copy = pltpu.make_async_remote_copy(
            src_ref=src, dst_ref=dst, send_sem=send_sem, recv_sem=recv_sem,
            device_id=target, device_id_type=MESH,
        )
        copy.start()
        return copy

    halos, moves, returns, owns = [], [], [], []
    for q in range(chunks):
        lanes = slice(256 * q, 256 * q + 256)
        table, outgoing = tables[q], halo_out[q]

        def fill(e, carry):
            got = jnp.dot(select_ref[...], dist_ref[e, :, lanes], preferred_element_type=jnp.float32)
            table[pl.ds(6 * e, 6)] = got.astype(low).reshape(6, 16, 256)
            return carry

        lax.fori_loop(0, elements, fill, 0)
        for j in range(2):

            def pick(m, carry):
                live = (m < count_ref[j]).astype(low)
                outgoing[slots * j + m] = table[send_ref[j, m]] * live
                return carry

            lax.fori_loop(0, slots, pick, 0)
        if q == 0:
            pl.semaphore_wait(barrier, ranks + 1)
        for j, target in ((1, after), (0, before)):
            halos.append(
                send(
                    outgoing.at[pl.ds(slots * j, slots)],
                    halo_in[q].at[pl.ds(slots * (1 - j), slots)],
                    hs.at[q, j], hr.at[q, j], {"space": target},
                )
            )

    for q in range(chunks):
        lanes = slice(256 * q, 256 * q + 256)
        table, moved = tables[q], moved_out[q]
        halos[2 * q].wait_recv()
        halos[2 * q + 1].wait_recv()
        table[local : local + 2 * slots] = halo_in[q][...]

        def step(e, carry):
            here = dist_ref[e, :, lanes]
            block[0:64] = here
            for face in range(6):
                got = table[source_ref[e, face]] * mask_ref[face : face + 1, lanes]
                block[64 + 16 * face : 80 + 16 * face] = got
                block[160 + 16 * face : 176 + 16 * face] = got
            parts = jnp.dot(w_ref[e], block[...], preferred_element_type=jnp.float32)
            total = coef_ref[:, lanes] * here.astype(jnp.float32)
            for a in range(3):
                total = total + scale_ref[a : a + 1, lanes] * parts[64 * a : 64 * a + 64]
            moved[e] = total.astype(low)
            return carry

        lax.fori_loop(0, elements, step, 0)
        slot = me * chunks + q
        for k, peer in enumerate(peers):
            moves.append(
                send(
                    moved.at[pl.ds(peer * share, share)], gathered.at[slot],
                    us.at[k, q], ur.at[k, q], {"vel": peer},
                )
            )
        gathered[slot] = moved[pl.ds(me * share, share)]

    for copy in moves:
        copy.wait_recv()
    for x in range(share):

        def collide(g, carry):
            rows = pl.ds(pl.multiple_of(16 * g, 16), 16)
            values = gathered[:, x, rows, :].reshape(256, 256)
            got = collide_block(
                values, kernel_ref, pair_t_ref[...], pair_ref[...], outer_ref[...], outer_t_ref[...]
            )
            for s in range(ranks):
                for q in range(chunks):
                    at = 16 * (chunks * s + q)
                    mixed[s, x, rows, 256 * q : 256 * q + 256] = got[at : at + 16]
            return carry

        lax.fori_loop(0, 4, collide, 0)
        spot = me * share + x
        for k, peer in enumerate(peers):
            returns.append(
                send(mixed.at[peer, x], out_ref.at[spot], ms.at[k, x], mr.at[k, x], {"vel": peer})
            )
        own = pltpu.make_async_copy(mixed.at[me, x], out_ref.at[spot], own_sem.at[x])
        own.start()
        owns.append(own)

    for copy in halos + moves:
        copy.wait_send()
    for copy in returns:
        copy.wait()
    for copy in owns:
        copy.wait()


def on_device(dist, send_faces, send_count, source_face, subface, alpha, beta):
    low = jnp.bfloat16
    elements = dist.shape[0]
    vel_local = dist.shape[2]
    slots = send_faces.shape[2]
    ranks = lax.axis_size("vel")
    blocks = lax.axis_size("space")
    chunks = vel_local // 256
    share = elements // ranks
    smem = pl.BlockSpec(memory_space=pltpu.SMEM)
    vmem = pl.BlockSpec(memory_space=pltpu.VMEM)
    stacked, selector = face_parts()

    speeds = velocity_components(lax.axis_index("vel") * vel_local, vel_local)
    column_level = jnp.concatenate(
        [jnp.zeros((elements, 64), subface.dtype)] + [jnp.repeat(subface, 16, axis=1)] * 2, axis=1
    )
    weights = jnp.zeros((elements, 192, 256), low)
    for level in range(stacked.shape[0]):
        weights = jnp.where(
            column_level[:, None, :] == level, jnp.asarray(stacked[level], low)[None], weights
        )
    digits = np.stack([np.arange(64) // 16, np.arange(64) // 4 % 4, np.arange(64) % 4])
    first = jnp.asarray(digits == 0, jnp.float32)[:, :, None]
    last = jnp.asarray(digits == 3, jnp.float32)[:, :, None]
    up = jnp.maximum(speeds, 0.0)[:, None, :]
    down = jnp.minimum(speeds, 0.0)[:, None, :]
    coef = 1.0 + courant * lift_weight * jnp.sum(last * down - first * up, axis=0)
    mask = jnp.stack(
        [-(speeds > 0).astype(low), (speeds < 0).astype(low)], axis=1
    ).reshape(6, vel_local)
    scale = -courant * speeds

    cosine = cosine_table()
    pair = np.kron(cosine, cosine)
    outer = np.kron(cosine, np.eye(16))
    tables = [jnp.asarray(t, low) for t in (pair.T, pair, outer, outer.T)]
    kernels = jnp.concatenate([alpha, beta], axis=0)
    kernels = kernels.reshape(kernels.shape[0], VSIDE, VSIDE * VSIDE)

    scratch = (
        [pltpu.VMEM((6 * elements + 2 * slots, 16, 256), low)] * chunks
        + [pltpu.VMEM((2 * slots, 16, 256), low)] * (2 * chunks)
        + [pltpu.VMEM((elements, 64, 256), low)] * chunks
        + [
            pltpu.VMEM((256, 256), low),
            pltpu.VMEM((ranks * chunks, share, 64, 256), low),
            pltpu.VMEM((ranks, share, 64, vel_local), low),
            pltpu.SemaphoreType.DMA((chunks, 2)),
            pltpu.SemaphoreType.DMA((chunks, 2)),
            pltpu.SemaphoreType.DMA((ranks - 1, chunks)),
            pltpu.SemaphoreType.DMA((ranks - 1, chunks)),
            pltpu.SemaphoreType.DMA((ranks - 1, share)),
            pltpu.SemaphoreType.DMA((ranks - 1, share)),
            pltpu.SemaphoreType.DMA((share,)),
        ]
    )
    return pl.pallas_call(
        functools.partial(fused_kernel, (chunks, ranks, blocks, slots)),
        out_shape=jax.ShapeDtypeStruct(dist.shape, low),
        in_specs=[smem] * 3 + [vmem] * 11,
        out_specs=pl.BlockSpec(memory_space=pl.ANY),
        scratch_shapes=scratch,
        compiler_params=pltpu.CompilerParams(
            collective_id=0, has_side_effects=True, vmem_limit_bytes=48 * 1024 * 1024
        ),
    )(
        send_faces[0], send_count[0], source_face, dist, jnp.asarray(selector, low), weights, coef,
        scale, mask, kernels, *tables,
    )


def solution(mesh):
    return jax.shard_map(
        on_device,
        mesh=mesh,
        in_specs=(
            P("space", None, "vel"),
            P("space", None, None),
            P("space", None),
            P("space", None),
            P("space", None),
            P(),
            P(),
        ),
        out_specs=P("space", None, "vel"),
        check_vma=False,
    )
```

```python
import functools

import jax
import jax.numpy as jnp
import numpy as np
from jax import lax
from jax.experimental import pallas as pl
from jax.experimental.pallas import tpu as pltpu
from jax.sharding import PartitionSpec as P

VSIDE = 16
VEL = 4096


courant = 0.1
lift_weight = 6.0
relax_step = 0.5
MESH = pl.DeviceIdType.MESH


def lobatto_points():
    return np.array([-1.0, -1.0 / np.sqrt(5.0), 1.0 / np.sqrt(5.0), 1.0])


def lagrange_table(targets):
    points = lobatto_points()
    result = np.ones((targets.shape[0], 4))
    for column in range(4):
        for second in range(4):
            if second != column:
                result[:, column] = (
                    result[:, column]
                    * (targets - points[second])
                    / (points[column] - points[second])
                )
    return result


def derivative_table():
    points = lobatto_points()
    result = np.zeros((4, 4))
    for row_at in range(4):
        for column in range(4):
            total = 0.0
            for skipped in range(4):
                if skipped != column:
                    factor = 1.0 / (points[column] - points[skipped])
                    for second in range(4):
                        if second != column and second != skipped:
                            factor = (
                                factor
                                * (points[row_at] - points[second])
                                / (points[column] - points[second])
                            )
                    total = total + factor
            result[row_at, column] = total
    return result


def cosine_table():
    index_list = np.arange(VSIDE)
    result = np.sqrt(2.0 / VSIDE) * np.cos(
        np.pi * (index_list[None, :] + 0.5) * index_list[:, None] / VSIDE
    )
    result[0] = result[0] / np.sqrt(2.0)
    return result


def static_tables():
    derivative = derivative_table()
    eye_four = np.eye(4)
    gradients = np.stack(
        [
            np.kron(np.kron(derivative, eye_four), eye_four),
            np.kron(np.kron(eye_four, derivative), eye_four),
            np.kron(np.kron(eye_four, eye_four), derivative),
        ]
    )
    selector = np.zeros((96, 64))
    for axis_at in range(3):
        for side_at in range(2):
            filled = 0
            for node_at in range(64):
                digits = (node_at // 16, node_at // 4 % 4, node_at % 4)
                if digits[axis_at] == 3 * side_at:
                    selector[(2 * axis_at + side_at) * 16 + filled, node_at] = 1.0
                    filled = filled + 1
    points = lobatto_points()
    halves = [lagrange_table((points - 1.0) / 2.0), lagrange_table((points + 1.0) / 2.0)]
    mortar = np.stack(
        [np.eye(16)]
        + [np.kron(halves[(which - 1) // 2], halves[(which - 1) % 2]) for which in range(1, 5)]
    )
    return (gradients, selector, mortar)


def face_parts():
    gradients, selector, mortar = static_tables()
    low = jnp.bfloat16
    grad = np.asarray(gradients.reshape(192, 64).astype(low), np.float64)
    mort = np.asarray(mortar.astype(low), np.float64)
    levels = mort.shape[0]
    spread = np.zeros((levels, 192, 96))
    for face in range(6):
        sel = selector[16 * face : 16 * face + 16]
        for level in range(levels):
            spread[level, 64 * (face // 2) : 64 * (face // 2) + 64, 16 * face : 16 * face + 16] = (
                sel.T @ mort[level]
            )
    stacked = np.concatenate(
        [np.broadcast_to(grad, (levels, 192, 64)), 4.0 * spread, 2.0 * spread], axis=2
    )
    return stacked, selector


def collide_block(values, kernels, pair_t, pair, outer, outer_t):
    low = jnp.bfloat16
    inner = jnp.dot(values, pair_t, preferred_element_type=jnp.float32).astype(low)
    spectrum = jnp.dot(outer, inner, preferred_element_type=jnp.float32).reshape(16, 16, 256)
    rows = kernels.shape[0]
    modes = (rows - 1) // 2

    def field(m):
        scaled = (spectrum * kernels[m][:, None, :]).astype(low).reshape(256, 256)
        back = jnp.dot(scaled, pair, preferred_element_type=jnp.float32).astype(low)
        return jnp.dot(outer_t, back, preferred_element_type=jnp.float32)

    wide = values.astype(jnp.float32)
    total = -wide * field(2 * modes)
    for m in range(modes):
        total = total + field(m) * field(modes + m)
    return (wide + relax_step * total).astype(low)


def fused_kernel(
    sizes, send_ref, count_ref, source_ref, level_ref, dist_hbm, select_ref, stack_hbm, alpha_ref,
    beta_ref, tables_hbm, out_ref, *scratch,
):
    chunks, ranks, blocks, slots = sizes
    tables, halo_out, halo_in, moved_out = (
        scratch[chunks * k : chunks * k + chunks] for k in range(4)
    )
    rest = scratch[4 * chunks :]
    block, gathered, mixed, dist_ref, stack_ref, turn_ref = rest[:6]
    w_ref, coef_ref, line_ref, kernel_ref = rest[6:10]
    hs, hr, us, ur, ls, lr, ms, mr, own_sem, in_sem = rest[10:]
    elements, _, width = dist_ref.shape
    share = elements // ranks
    local = 6 * elements
    low = jnp.bfloat16
    place = lax.axis_index("space")
    me = lax.axis_index("vel")
    after = lax.rem(place + 1, blocks)
    before = lax.rem(place + blocks - 1, blocks)
    peers = [lax.rem(me + k, ranks) for k in range(1, ranks)]

    barrier = pltpu.get_barrier_semaphore()
    for other in (before, after):
        pl.semaphore_signal(barrier, inc=1, device_id={"space": other}, device_id_type=MESH)
    for peer in peers:
        pl.semaphore_signal(barrier, inc=1, device_id={"vel": peer}, device_id_type=MESH)

    loads = [
        pltpu.make_async_copy(
            dist_hbm.at[:, :, pl.ds(256 * q, 256)], dist_ref.at[:, :, pl.ds(256 * q, 256)],
            in_sem.at[q],
        )
        for q in range(chunks)
    ]
    loads.append(pltpu.make_async_copy(stack_hbm, stack_ref, in_sem.at[chunks]))
    loads.append(pltpu.make_async_copy(tables_hbm, turn_ref, in_sem.at[chunks + 1]))
    for copy in loads:
        copy.start()

    def remote(src, dst, send_sem, recv_sem, target):
        return pltpu.make_async_remote_copy(
            src_ref=src, dst_ref=dst, send_sem=send_sem, recv_sem=recv_sem,
            device_id=target, device_id_type=MESH,
        )

    def send(*args):
        copy = remote(*args)
        copy.start()
        return copy

    halos, moves, lasts = [], [], []
    for q in range(chunks):
        lanes = slice(256 * q, 256 * q + 256)
        table, outgoing = tables[q], halo_out[q]
        loads[q].wait()

        def fill(e, carry):
            got = jnp.dot(select_ref[...], dist_ref[e, :, lanes], preferred_element_type=jnp.float32)
            table[pl.ds(6 * e, 6)] = got.astype(low).reshape(6, 16, 256)
            return carry

        lax.fori_loop(0, elements, fill, 0)
        for j in range(2):

            def pick(m, carry):
                live = (m < count_ref[0, j]).astype(low)
                outgoing[slots * j + m] = table[send_ref[0, j, m]] * live
                return carry

            lax.fori_loop(0, slots, pick, 0)
        if q == 0:
            pl.semaphore_wait(barrier, ranks + 1)
        for j, target in ((1, after), (0, before)):
            halos.append(
                send(
                    outgoing.at[pl.ds(slots * j, slots)],
                    halo_in[q].at[pl.ds(slots * (1 - j), slots)],
                    hs.at[q, j], hr.at[q, j], {"space": target},
                )
            )

    index = lax.broadcasted_iota(jnp.int32, (1, width), 1) + me * width
    node = lax.broadcasted_iota(jnp.int32, (64, width), 0)
    coef = jnp.ones((64, width), jnp.float32)
    for a in range(3):
        along = lax.shift_right_logical(index, 8 - 4 * a) & 15
        speed = (along.astype(jnp.float32) + 0.5) * (2.0 / VSIDE) - 1.0
        up, down = jnp.maximum(speed, 0.0), jnp.minimum(speed, 0.0)
        line_ref[2 * a : 2 * a + 1, :] = jnp.where(speed > 0, -1.0, 0.0)
        line_ref[2 * a + 1 : 2 * a + 2, :] = jnp.where(speed < 0, 1.0, 0.0)
        line_ref[8 + a : 9 + a, :] = -courant * speed
        digit = lax.shift_right_logical(node, 4 - 2 * a) & 3
        inflow = jnp.where(digit == 3, down, 0.0) - jnp.where(digit == 0, up, 0.0)
        coef = coef + courant * lift_weight * inflow
    coef_ref[...] = coef
    modes = alpha_ref.shape[0]
    for m in range(2 * modes + 1):
        source, row = (alpha_ref, m) if m < modes else (beta_ref, m - modes)
        for i in range(VSIDE):
            kernel_ref[m, i : i + 1, :] = source[row : row + 1, 256 * i : 256 * i + 256]
    loads[chunks].wait()
    lane = lax.broadcasted_iota(jnp.int32, (1, 256), 1)
    shifted = jnp.where(lane >= 160, lane - 160, lane - 64)
    column = lax.shift_right_arithmetic(shifted, 4)

    def weigh(e, carry):
        level = jnp.zeros((1, 256), jnp.int32)
        for face in range(6):
            level = jnp.where(column == face, level_ref[face, e], level)
        total = stack_ref[0] * (level == 0).astype(jnp.float32).astype(low)
        for k in range(1, 5):
            total = total + stack_ref[k] * (level == k).astype(jnp.float32).astype(low)
        w_ref[e] = total
        return carry

    lax.fori_loop(0, elements, weigh, 0)
    loads[chunks + 1].wait()

    for q in range(chunks):
        lanes = slice(256 * q, 256 * q + 256)
        table, moved = tables[q], moved_out[q]
        halos[2 * q].wait_recv()
        halos[2 * q + 1].wait_recv()
        table[local : local + 2 * slots] = halo_in[q][...]

        def step(e, carry):
            here = dist_ref[e, :, lanes]
            block[0:64] = here
            for face in range(6):
                got = table[source_ref[face, e]] * line_ref[face : face + 1, lanes].astype(low)
                block[64 + 16 * face : 80 + 16 * face] = got
                block[160 + 16 * face : 176 + 16 * face] = got
            parts = jnp.dot(w_ref[e], block[...], preferred_element_type=jnp.float32)
            total = coef_ref[:, lanes] * here.astype(jnp.float32)
            for a in range(3):
                total = total + line_ref[8 + a : 9 + a, lanes] * parts[64 * a : 64 * a + 64]
            moved[e] = total.astype(low)
            return carry

        lax.fori_loop(0, elements, step, 0)
        slot = me * chunks + q
        if q < chunks - 1:
            for k, peer in enumerate(peers):
                moves.append(
                    send(
                        moved.at[pl.ds(peer * share, share)], gathered.at[slot],
                        us.at[k, q], ur.at[k, q], {"vel": peer},
                    )
                )
        else:
            for x in range(share):
                for k, peer in enumerate(peers):
                    lasts.append(
                        send(
                            moved.at[peer * share + x], gathered.at[slot, x],
                            ls.at[k, x], lr.at[k, x], {"vel": peer},
                        )
                    )
        gathered[slot] = moved[pl.ds(me * share, share)]

    def returned(k, x, g):
        rows = pl.ds(pl.multiple_of(16 * g, 16), 16)
        return remote(
            mixed.at[peers[k], x, rows], out_ref.at[me * share + x, rows],
            ms.at[k, x, g], mr.at[k, x, g], {"vel": peers[k]},
        )

    def kept(x, g):
        rows = pl.ds(pl.multiple_of(16 * g, 16), 16)
        return pltpu.make_async_copy(
            mixed.at[me, x, rows], out_ref.at[me * share + x, rows], own_sem.at[x, g]
        )

    for copy in moves:
        copy.wait_recv()
    for x in range(share):
        for k in range(ranks - 1):
            lasts[(ranks - 1) * x + k].wait_recv()

        def collide(g, carry):
            rows = pl.ds(pl.multiple_of(16 * g, 16), 16)
            values = gathered[:, x, rows, :].reshape(256, 256)
            got = collide_block(
                values, kernel_ref, turn_ref[0], turn_ref[1], turn_ref[2], turn_ref[3]
            )
            for s in range(ranks):
                for q in range(chunks):
                    at = 16 * (chunks * s + q)
                    mixed[s, x, rows, 256 * q : 256 * q + 256] = got[at : at + 16]
            for k in range(ranks - 1):
                returned(k, x, g).start()
            kept(x, g).start()
            return carry

        lax.fori_loop(0, 4, collide, 0)

    for copy in halos + moves + lasts:
        copy.wait_send()

    def finish(g, carry):
        for x in range(share):
            for k in range(ranks - 1):
                returned(k, x, g).wait()
            kept(x, g).wait()
        return carry

    lax.fori_loop(0, 4, finish, 0)


def on_device(dist, send_faces, send_count, source_face, subface, alpha, beta):
    low = jnp.bfloat16
    elements, _, vel_local = dist.shape
    slots = send_faces.shape[2]
    ranks = lax.axis_size("vel")
    blocks = lax.axis_size("space")
    chunks = vel_local // 256
    share = elements // ranks
    rows = alpha.shape[0] + beta.shape[0]
    smem = pl.BlockSpec(memory_space=pltpu.SMEM)
    vmem = pl.BlockSpec(memory_space=pltpu.VMEM)
    anywhere = pl.BlockSpec(memory_space=pl.ANY)
    stacked, selector = face_parts()
    cosine = cosine_table()
    pair = np.kron(cosine, cosine)
    outer = np.kron(cosine, np.eye(16))
    turns = np.stack([pair.T, pair, outer, outer.T])

    dma = pltpu.SemaphoreType.DMA
    scratch = (
        [pltpu.VMEM((6 * elements + 2 * slots, 16, 256), low)] * chunks
        + [pltpu.VMEM((2 * slots, 16, 256), low)] * (2 * chunks)
        + [pltpu.VMEM((elements, 64, 256), low)] * chunks
        + [
            pltpu.VMEM((256, 256), low),
            pltpu.VMEM((ranks * chunks, share, 64, 256), low),
            pltpu.VMEM((ranks, share, 64, vel_local), low),
            pltpu.VMEM(dist.shape, low),
            pltpu.VMEM(stacked.shape, low),
            pltpu.VMEM(turns.shape, low),
            pltpu.VMEM((elements, 192, 256), low),
            pltpu.VMEM((64, vel_local), jnp.float32),
            pltpu.VMEM((16, vel_local), jnp.float32),
            pltpu.VMEM((rows, VSIDE, 256), jnp.float32),
        ]
        + [dma((chunks, 2))] * 2
        + [dma((ranks - 1, chunks))] * 2
        + [dma((ranks - 1, share))] * 2
        + [dma((ranks - 1, share, 4))] * 2
        + [dma((share, 4)), dma((chunks + 2,))]
    )
    return pl.pallas_call(
        functools.partial(fused_kernel, (chunks, ranks, blocks, slots)),
        out_shape=jax.ShapeDtypeStruct(dist.shape, low),
        in_specs=[smem] * 4 + [anywhere, vmem, anywhere, vmem, vmem, anywhere],
        out_specs=anywhere,
        scratch_shapes=scratch,
        compiler_params=pltpu.CompilerParams(
            collective_id=0, has_side_effects=True, vmem_limit_bytes=56 * 1024 * 1024
        ),
    )(
        send_faces, send_count, source_face.T, subface.T, dist, jnp.asarray(selector, low),
        jnp.asarray(stacked, low), alpha, beta, jnp.asarray(turns, low),
    )


def solution(mesh):
    return jax.shard_map(
        on_device,
        mesh=mesh,
        in_specs=(
            P("space", None, "vel"),
            P("space", None, None),
            P("space", None),
            P("space", None),
            P("space", None),
            P(),
            P(),
        ),
        out_specs=P("space", None, "vel"),
        check_vma=False,
    )
```

```python
import functools

import jax
import jax.numpy as jnp
import numpy as np
from jax import lax
from jax.experimental import pallas as pl
from jax.experimental.pallas import tpu as pltpu
from jax.sharding import PartitionSpec as P

VSIDE = 16
VEL = 4096


courant = 0.1
lift_weight = 6.0
relax_step = 0.5
MESH = pl.DeviceIdType.MESH


def lobatto_points():
    return np.array([-1.0, -1.0 / np.sqrt(5.0), 1.0 / np.sqrt(5.0), 1.0])


def lagrange_table(targets):
    points = lobatto_points()
    result = np.ones((targets.shape[0], 4))
    for column in range(4):
        for second in range(4):
            if second != column:
                result[:, column] = (
                    result[:, column]
                    * (targets - points[second])
                    / (points[column] - points[second])
                )
    return result


def derivative_table():
    points = lobatto_points()
    result = np.zeros((4, 4))
    for row_at in range(4):
        for column in range(4):
            total = 0.0
            for skipped in range(4):
                if skipped != column:
                    factor = 1.0 / (points[column] - points[skipped])
                    for second in range(4):
                        if second != column and second != skipped:
                            factor = (
                                factor
                                * (points[row_at] - points[second])
                                / (points[column] - points[second])
                            )
                    total = total + factor
            result[row_at, column] = total
    return result


def cosine_table():
    index_list = np.arange(VSIDE)
    result = np.sqrt(2.0 / VSIDE) * np.cos(
        np.pi * (index_list[None, :] + 0.5) * index_list[:, None] / VSIDE
    )
    result[0] = result[0] / np.sqrt(2.0)
    return result


def static_tables():
    derivative = derivative_table()
    eye_four = np.eye(4)
    gradients = np.stack(
        [
            np.kron(np.kron(derivative, eye_four), eye_four),
            np.kron(np.kron(eye_four, derivative), eye_four),
            np.kron(np.kron(eye_four, eye_four), derivative),
        ]
    )
    selector = np.zeros((96, 64))
    for axis_at in range(3):
        for side_at in range(2):
            filled = 0
            for node_at in range(64):
                digits = (node_at // 16, node_at // 4 % 4, node_at % 4)
                if digits[axis_at] == 3 * side_at:
                    selector[(2 * axis_at + side_at) * 16 + filled, node_at] = 1.0
                    filled = filled + 1
    points = lobatto_points()
    halves = [lagrange_table((points - 1.0) / 2.0), lagrange_table((points + 1.0) / 2.0)]
    mortar = np.stack(
        [np.eye(16)]
        + [np.kron(halves[(which - 1) // 2], halves[(which - 1) % 2]) for which in range(1, 5)]
    )
    return (gradients, selector, mortar)


def face_parts():
    gradients, selector, mortar = static_tables()
    low = jnp.bfloat16
    grad = np.asarray(gradients.reshape(192, 64).astype(low), np.float64)
    mort = np.asarray(mortar.astype(low), np.float64)
    levels = mort.shape[0]
    spread = np.zeros((levels, 192, 96))
    for face in range(6):
        sel = selector[16 * face : 16 * face + 16]
        for level in range(levels):
            spread[level, 64 * (face // 2) : 64 * (face // 2) + 64, 16 * face : 16 * face + 16] = (
                sel.T @ mort[level]
            )
    stacked = np.concatenate(
        [np.broadcast_to(grad, (levels, 192, 64)), 4.0 * spread, 2.0 * spread], axis=2
    )
    return stacked, selector


def collide_block(values, kernels, pair_t, pair, outer, outer_t):
    low = jnp.bfloat16
    inner = jnp.dot(values, pair_t, preferred_element_type=jnp.float32).astype(low)
    spectrum = jnp.dot(outer, inner, preferred_element_type=jnp.float32).reshape(16, 16, 256)
    rows = kernels.shape[0]
    modes = (rows - 1) // 2

    def field(m):
        scaled = (spectrum * kernels[m][:, None, :]).astype(low).reshape(256, 256)
        back = jnp.dot(scaled, pair, preferred_element_type=jnp.float32).astype(low)
        return jnp.dot(outer_t, back, preferred_element_type=jnp.float32)

    wide = values.astype(jnp.float32)
    total = -wide * field(2 * modes)
    for m in range(modes):
        total = total + field(m) * field(modes + m)
    return (wide + relax_step * total).astype(low)


def fused_kernel(
    sizes, send_ref, count_ref, source_ref, level_ref, dist_hbm, select_ref, stack_hbm, alpha_ref,
    beta_ref, tables_hbm, out_ref, *scratch,
):
    spans, ranks, blocks, slots = sizes
    chunks = len(spans)
    tables, halo_out, halo_in, moved_out = (
        scratch[chunks * k : chunks * k + chunks] for k in range(4)
    )
    rest = scratch[4 * chunks :]
    gathered, mixed, dist_ref, stack_ref, turn_ref = rest[:5]
    w_ref, coef_ref, line_ref, kernel_ref = rest[5:9]
    hs, hr, us, ur, ls, lr, ms, mr, own_sem, in_sem = rest[9:]
    elements, _, width = dist_ref.shape
    share = elements // ranks
    groups = width // 256
    local = 6 * elements
    low = jnp.bfloat16
    place = lax.axis_index("space")
    me = lax.axis_index("vel")
    after = lax.rem(place + 1, blocks)
    before = lax.rem(place + blocks - 1, blocks)
    peers = [lax.rem(me + k, ranks) for k in range(1, ranks)]

    barrier = pltpu.get_barrier_semaphore()
    for other in (before, after):
        pl.semaphore_signal(barrier, inc=1, device_id={"space": other}, device_id_type=MESH)
    for peer in peers:
        pl.semaphore_signal(barrier, inc=1, device_id={"vel": peer}, device_id_type=MESH)

    loads = [
        pltpu.make_async_copy(
            dist_hbm.at[:, :, pl.ds(at, wide)], dist_ref.at[:, :, pl.ds(at, wide)], in_sem.at[q]
        )
        for q, (at, wide) in enumerate(spans)
    ]
    loads.append(pltpu.make_async_copy(stack_hbm, stack_ref, in_sem.at[chunks]))
    loads.append(pltpu.make_async_copy(tables_hbm, turn_ref, in_sem.at[chunks + 1]))
    for copy in loads:
        copy.start()

    def remote(src, dst, send_sem, recv_sem, target):
        return pltpu.make_async_remote_copy(
            src_ref=src, dst_ref=dst, send_sem=send_sem, recv_sem=recv_sem,
            device_id=target, device_id_type=MESH,
        )

    def send(*args):
        copy = remote(*args)
        copy.start()
        return copy

    halos, moves, lasts = [], [], []

    def start_halo(q):
        at, wide = spans[q]
        lanes = slice(at, at + wide)
        table, outgoing = tables[q], halo_out[q]
        loads[q].wait()

        def fill(e, carry):
            got = jnp.dot(select_ref[...], dist_ref[e, :, lanes], preferred_element_type=jnp.float32)
            table[pl.ds(6 * e, 6)] = got.astype(low).reshape(6, 16, wide)
            return carry

        lax.fori_loop(0, elements, fill, 0, unroll=4)
        for j in range(2):

            def pick(m, carry):
                live = (m < count_ref[0, j]).astype(low)
                outgoing[slots * j + m] = table[send_ref[0, j, m]] * live
                return carry

            lax.fori_loop(0, slots, pick, 0, unroll=4)
        if q == 0:
            pl.semaphore_wait(barrier, ranks + 1)
        for j, target in ((1, after), (0, before)):
            halos.append(
                send(
                    outgoing.at[pl.ds(slots * j, slots)],
                    halo_in[q].at[pl.ds(slots * (1 - j), slots)],
                    hs.at[q, j], hr.at[q, j], {"space": target},
                )
            )

    def transport(q):
        at, wide = spans[q]
        lanes = slice(at, at + wide)
        table, moved = tables[q], moved_out[q]
        halos[2 * q].wait_recv()
        halos[2 * q + 1].wait_recv()
        table[local : local + 2 * slots] = halo_in[q][...]
        signs = [line_ref[face : face + 1, lanes].astype(low) for face in range(6)]

        def step(e, carry):
            here = dist_ref[e, :, lanes]
            near = [table[source_ref[face, e]] * signs[face] for face in range(6)]
            stacked = jnp.concatenate([here] + near + near, axis=0)
            parts = jnp.dot(w_ref[e], stacked, preferred_element_type=jnp.float32)
            total = coef_ref[:, lanes] * here.astype(jnp.float32)
            for a in range(3):
                total = total + line_ref[8 + a : 9 + a, lanes] * parts[64 * a : 64 * a + 64]
            moved[e] = total.astype(low)
            return carry

        lax.fori_loop(0, elements, step, 0, unroll=2)
        slot = me * groups + at // 256
        inside = pl.ds(at % 256, wide)
        if q < chunks - 1:
            for k, peer in enumerate(peers):
                moves.append(
                    send(
                        moved.at[pl.ds(peer * share, share)], gathered.at[slot, :, :, inside],
                        us.at[k, q], ur.at[k, q], {"vel": peer},
                    )
                )
        else:
            for x in range(share):
                for k, peer in enumerate(peers):
                    lasts.append(
                        send(
                            moved.at[peer * share + x], gathered.at[slot, x, :, inside],
                            ls.at[k, x], lr.at[k, x], {"vel": peer},
                        )
                    )
        gathered[slot, :, :, at % 256 : at % 256 + wide] = moved[pl.ds(me * share, share)]

    ahead = min(3, chunks)
    for q in range(ahead):
        start_halo(q)

    index = lax.broadcasted_iota(jnp.int32, (1, width), 1) + me * width
    node = lax.broadcasted_iota(jnp.int32, (64, width), 0)
    coef = jnp.ones((64, width), jnp.float32)
    for a in range(3):
        along = lax.shift_right_logical(index, 8 - 4 * a) & 15
        speed = (along.astype(jnp.float32) + 0.5) * (2.0 / VSIDE) - 1.0
        up, down = jnp.maximum(speed, 0.0), jnp.minimum(speed, 0.0)
        line_ref[2 * a : 2 * a + 1, :] = jnp.where(speed > 0, -1.0, 0.0)
        line_ref[2 * a + 1 : 2 * a + 2, :] = jnp.where(speed < 0, 1.0, 0.0)
        line_ref[8 + a : 9 + a, :] = -courant * speed
        digit = lax.shift_right_logical(node, 4 - 2 * a) & 3
        inflow = jnp.where(digit == 3, down, 0.0) - jnp.where(digit == 0, up, 0.0)
        coef = coef + courant * lift_weight * inflow
    coef_ref[...] = coef
    modes = alpha_ref.shape[0]
    for m in range(2 * modes + 1):
        source, row = (alpha_ref, m) if m < modes else (beta_ref, m - modes)
        for i in range(VSIDE):
            kernel_ref[m, i : i + 1, :] = source[row : row + 1, 256 * i : 256 * i + 256]
    loads[chunks].wait()
    lane = lax.broadcasted_iota(jnp.int32, (1, 256), 1)
    shifted = jnp.where(lane >= 160, lane - 160, lane - 64)
    column = lax.shift_right_arithmetic(shifted, 4)

    def weigh(e, carry):
        level = jnp.zeros((1, 256), jnp.int32)
        for face in range(6):
            level = jnp.where(column == face, level_ref[face, e], level)
        total = stack_ref[0] * (level == 0).astype(jnp.float32).astype(low)
        for k in range(1, 5):
            total = total + stack_ref[k] * (level == k).astype(jnp.float32).astype(low)
        w_ref[e] = total
        return carry

    lax.fori_loop(0, elements, weigh, 0, unroll=2)
    loads[chunks + 1].wait()

    for q in range(chunks):
        transport(q)
        if q + ahead < chunks:
            start_halo(q + ahead)

    def returned(k, x, g):
        rows = pl.ds(pl.multiple_of(16 * g, 16), 16)
        return remote(
            mixed.at[peers[k], x, rows], out_ref.at[me * share + x, rows],
            ms.at[k, x, g], mr.at[k, x, g], {"vel": peers[k]},
        )

    def kept(x, g):
        rows = pl.ds(pl.multiple_of(16 * g, 16), 16)
        return pltpu.make_async_copy(
            mixed.at[me, x, rows], out_ref.at[me * share + x, rows], own_sem.at[x, g]
        )

    for copy in moves:
        copy.wait_recv()
    for x in range(share):
        for k in range(ranks - 1):
            lasts[(ranks - 1) * x + k].wait_recv()

        def collide(g, carry):
            rows = pl.ds(pl.multiple_of(16 * g, 16), 16)
            values = gathered[:, x, rows, :].reshape(256, 256)
            got = collide_block(
                values, kernel_ref, turn_ref[0], turn_ref[1], turn_ref[2], turn_ref[3]
            )
            for s in range(ranks):
                for q in range(groups):
                    at = 16 * (groups * s + q)
                    mixed[s, x, rows, 256 * q : 256 * q + 256] = got[at : at + 16]
            for k in range(ranks - 1):
                returned(k, x, g).start()
            kept(x, g).start()
            return carry

        lax.fori_loop(0, 4, collide, 0)

    for copy in halos + moves + lasts:
        copy.wait_send()

    def finish(g, carry):
        for x in range(share):
            for k in range(ranks - 1):
                returned(k, x, g).wait()
            kept(x, g).wait()
        return carry

    lax.fori_loop(0, 4, finish, 0)


def on_device(dist, send_faces, send_count, source_face, subface, alpha, beta):
    low = jnp.bfloat16
    elements, _, vel_local = dist.shape
    slots = send_faces.shape[2]
    ranks = lax.axis_size("vel")
    blocks = lax.axis_size("space")
    spans = [(0, 128), (128, 128)] + [(at, 256) for at in range(256, vel_local, 256)]
    chunks = len(spans)
    share = elements // ranks
    rows = alpha.shape[0] + beta.shape[0]
    smem = pl.BlockSpec(memory_space=pltpu.SMEM)
    vmem = pl.BlockSpec(memory_space=pltpu.VMEM)
    anywhere = pl.BlockSpec(memory_space=pl.ANY)
    hbm = pl.BlockSpec(memory_space=pltpu.HBM)
    stacked, selector = face_parts()
    cosine = cosine_table()
    pair = np.kron(cosine, cosine)
    outer = np.kron(cosine, np.eye(16))
    turns = np.stack([pair.T, pair, outer, outer.T])

    dma = pltpu.SemaphoreType.DMA
    scratch = (
        [pltpu.VMEM((6 * elements + 2 * slots, 16, wide), low) for _, wide in spans]
        + [pltpu.VMEM((2 * slots, 16, wide), low) for _, wide in spans] * 2
        + [pltpu.VMEM((elements, 64, wide), low) for _, wide in spans]
        + [
            pltpu.VMEM((ranks * vel_local // 256, share, 64, 256), low),
            pltpu.VMEM((ranks, share, 64, vel_local), low),
            pltpu.VMEM(dist.shape, low),
            pltpu.VMEM(stacked.shape, low),
            pltpu.VMEM(turns.shape, low),
            pltpu.VMEM((elements, 192, 256), low),
            pltpu.VMEM((64, vel_local), jnp.float32),
            pltpu.VMEM((16, vel_local), jnp.float32),
            pltpu.VMEM((rows, VSIDE, 256), jnp.float32),
        ]
        + [dma((chunks, 2))] * 2
        + [dma((ranks - 1, chunks))] * 2
        + [dma((ranks - 1, share))] * 2
        + [dma((ranks - 1, share, 4))] * 2
        + [dma((share, 4)), dma((chunks + 2,))]
    )
    return pl.pallas_call(
        functools.partial(fused_kernel, (spans, ranks, blocks, slots)),
        out_shape=jax.ShapeDtypeStruct(dist.shape, low),
        in_specs=[smem] * 4 + [hbm, vmem, hbm, vmem, vmem, hbm],
        out_specs=anywhere,
        scratch_shapes=scratch,
        compiler_params=pltpu.CompilerParams(
            collective_id=0, has_side_effects=True, vmem_limit_bytes=56 * 1024 * 1024
        ),
    )(
        send_faces, send_count, source_face.T, subface.T, dist, jnp.asarray(selector, low),
        jnp.asarray(stacked, low), alpha, beta, jnp.asarray(turns, low),
    )


def solution(mesh):
    return jax.shard_map(
        on_device,
        mesh=mesh,
        in_specs=(
            P("space", None, "vel"),
            P("space", None, None),
            P("space", None),
            P("space", None),
            P("space", None),
            P(),
            P(),
        ),
        out_specs=P("space", None, "vel"),
        check_vma=False,
    )
```

```python
import functools

import jax
import jax.numpy as jnp
import numpy as np
from jax import lax
from jax.experimental import pallas as pl
from jax.experimental.pallas import tpu as pltpu
from jax.sharding import PartitionSpec as P

VSIDE = 16
VEL = 4096


courant = 0.1
lift_weight = 6.0
relax_step = 0.5
MESH = pl.DeviceIdType.MESH


def lobatto_points():
    return np.array([-1.0, -1.0 / np.sqrt(5.0), 1.0 / np.sqrt(5.0), 1.0])


def lagrange_table(targets):
    points = lobatto_points()
    result = np.ones((targets.shape[0], 4))
    for column in range(4):
        for second in range(4):
            if second != column:
                result[:, column] = (
                    result[:, column]
                    * (targets - points[second])
                    / (points[column] - points[second])
                )
    return result


def derivative_table():
    points = lobatto_points()
    result = np.zeros((4, 4))
    for row_at in range(4):
        for column in range(4):
            total = 0.0
            for skipped in range(4):
                if skipped != column:
                    factor = 1.0 / (points[column] - points[skipped])
                    for second in range(4):
                        if second != column and second != skipped:
                            factor = (
                                factor
                                * (points[row_at] - points[second])
                                / (points[column] - points[second])
                            )
                    total = total + factor
            result[row_at, column] = total
    return result


def cosine_table():
    index_list = np.arange(VSIDE)
    result = np.sqrt(2.0 / VSIDE) * np.cos(
        np.pi * (index_list[None, :] + 0.5) * index_list[:, None] / VSIDE
    )
    result[0] = result[0] / np.sqrt(2.0)
    return result


def static_tables():
    derivative = derivative_table()
    eye_four = np.eye(4)
    gradients = np.stack(
        [
            np.kron(np.kron(derivative, eye_four), eye_four),
            np.kron(np.kron(eye_four, derivative), eye_four),
            np.kron(np.kron(eye_four, eye_four), derivative),
        ]
    )
    selector = np.zeros((96, 64))
    for axis_at in range(3):
        for side_at in range(2):
            filled = 0
            for node_at in range(64):
                digits = (node_at // 16, node_at // 4 % 4, node_at % 4)
                if digits[axis_at] == 3 * side_at:
                    selector[(2 * axis_at + side_at) * 16 + filled, node_at] = 1.0
                    filled = filled + 1
    points = lobatto_points()
    halves = [lagrange_table((points - 1.0) / 2.0), lagrange_table((points + 1.0) / 2.0)]
    mortar = np.stack(
        [np.eye(16)]
        + [np.kron(halves[(which - 1) // 2], halves[(which - 1) % 2]) for which in range(1, 5)]
    )
    return (gradients, selector, mortar)


def face_parts():
    gradients, selector, mortar = static_tables()
    low = jnp.bfloat16
    grad = np.asarray(gradients.reshape(192, 64).astype(low), np.float64)
    mort = np.asarray(mortar.astype(low), np.float64)
    levels = mort.shape[0]
    spread = np.zeros((levels, 192, 96))
    for face in range(6):
        sel = selector[16 * face : 16 * face + 16]
        for level in range(levels):
            spread[level, 64 * (face // 2) : 64 * (face // 2) + 64, 16 * face : 16 * face + 16] = (
                sel.T @ mort[level]
            )
    stacked = np.concatenate(
        [np.broadcast_to(grad, (levels, 192, 64)), 4.0 * spread, 2.0 * spread], axis=2
    )
    return stacked, selector


def collide_block(values, kernels, pair_t, pair, outer, outer_t):
    low = jnp.bfloat16
    inner = jnp.dot(values, pair_t, preferred_element_type=jnp.float32).astype(low)
    spectrum = jnp.dot(outer, inner, preferred_element_type=jnp.float32).reshape(16, 16, 256)
    rows = kernels.shape[0]
    modes = (rows - 1) // 2

    def field(m):
        scaled = (spectrum * kernels[m][:, None, :]).astype(low).reshape(256, 256)
        back = jnp.dot(scaled, pair, preferred_element_type=jnp.float32).astype(low)
        return jnp.dot(outer_t, back, preferred_element_type=jnp.float32)

    wide = values.astype(jnp.float32)
    total = -wide * field(2 * modes)
    for m in range(modes):
        total = total + field(m) * field(modes + m)
    return (wide + relax_step * total).astype(low)


def fused_kernel(
    sizes, send_ref, count_ref, source_ref, level_ref, dist_hbm, select_ref, stack_hbm, alpha_ref,
    beta_ref, tables_hbm, out_ref, *scratch,
):
    spans, ranks, blocks, slots = sizes
    chunks = len(spans)
    tables, halo_out, halo_in, moved_out = (
        scratch[chunks * k : chunks * k + chunks] for k in range(4)
    )
    rest = scratch[4 * chunks :]
    gathered, mixed, dist_ref, stack_ref, turn_ref = rest[:5]
    w_ref, coef_ref, line_ref, kernel_ref = rest[5:9]
    hs, hr, us, ur, ls, lr, ms, mr, own_sem, in_sem = rest[9:]
    elements, _, width = dist_ref.shape
    share = elements // ranks
    groups = width // 256
    local = 6 * elements
    low = jnp.bfloat16
    place = lax.axis_index("space")
    me = lax.axis_index("vel")
    after = lax.rem(place + 1, blocks)
    before = lax.rem(place + blocks - 1, blocks)
    peers = [lax.rem(me + k, ranks) for k in range(1, ranks)]

    barrier = pltpu.get_barrier_semaphore()
    for other in (before, after):
        pl.semaphore_signal(barrier, inc=1, device_id={"space": other}, device_id_type=MESH)
    for peer in peers:
        pl.semaphore_signal(barrier, inc=1, device_id={"vel": peer}, device_id_type=MESH)

    loads = [
        pltpu.make_async_copy(
            dist_hbm.at[:, :, pl.ds(at, wide)], dist_ref.at[:, :, pl.ds(at, wide)], in_sem.at[q]
        )
        for q, (at, wide) in enumerate(spans)
    ]
    loads.append(pltpu.make_async_copy(stack_hbm, stack_ref, in_sem.at[chunks]))
    loads.append(pltpu.make_async_copy(tables_hbm, turn_ref, in_sem.at[chunks + 1]))
    for copy in loads:
        copy.start()

    def remote(src, dst, send_sem, recv_sem, target):
        return pltpu.make_async_remote_copy(
            src_ref=src, dst_ref=dst, send_sem=send_sem, recv_sem=recv_sem,
            device_id=target, device_id_type=MESH,
        )

    def send(*args):
        copy = remote(*args)
        copy.start()
        return copy

    halos, moves, lasts = [], [], []

    def start_halo(q):
        at, wide = spans[q]
        lanes = slice(at, at + wide)
        table, outgoing = tables[q], halo_out[q]
        loads[q].wait()

        def fill(e, carry):
            got = jnp.dot(select_ref[...], dist_ref[e, :, lanes], preferred_element_type=jnp.float32)
            table[pl.ds(6 * e, 6)] = got.astype(low).reshape(6, 16, wide)
            return carry

        lax.fori_loop(0, elements, fill, 0, unroll=4)
        for j in range(2):

            def pick(m, carry):
                live = (m < count_ref[0, j]).astype(low)
                outgoing[slots * j + m] = table[send_ref[0, j, m]] * live
                return carry

            lax.fori_loop(0, slots, pick, 0, unroll=4)
        if q == 0:
            pl.semaphore_wait(barrier, ranks + 1)
        for j, target in ((1, after), (0, before)):
            halos.append(
                send(
                    outgoing.at[pl.ds(slots * j, slots)],
                    halo_in[q].at[pl.ds(slots * (1 - j), slots)],
                    hs.at[q, j], hr.at[q, j], {"space": target},
                )
            )

    def transport(q):
        at, wide = spans[q]
        lanes = slice(at, at + wide)
        table, moved = tables[q], moved_out[q]
        halos[2 * q].wait_recv()
        halos[2 * q + 1].wait_recv()
        table[local : local + 2 * slots] = halo_in[q][...]
        signs = [line_ref[face : face + 1, lanes].astype(low) for face in range(6)]

        def step(e, carry):
            here = dist_ref[e, :, lanes]
            near = [table[source_ref[face, e]] * signs[face] for face in range(6)]
            stacked = jnp.concatenate([here] + near + near, axis=0)
            parts = jnp.dot(w_ref[e], stacked, preferred_element_type=jnp.float32)
            total = coef_ref[:, lanes] * here.astype(jnp.float32)
            for a in range(3):
                total = total + line_ref[8 + a : 9 + a, lanes] * parts[64 * a : 64 * a + 64]
            moved[e] = total.astype(low)
            return carry

        lax.fori_loop(0, elements, step, 0, unroll=2)
        slot = me * groups + at // 256
        inside = pl.ds(at % 256, wide)
        if q < chunks - 1:
            for k, peer in enumerate(peers):
                moves.append(
                    send(
                        moved.at[pl.ds(peer * share, share)], gathered.at[slot, :, :, inside],
                        us.at[k, q], ur.at[k, q], {"vel": peer},
                    )
                )
        else:
            for x in range(share):
                for k, peer in enumerate(peers):
                    lasts.append(
                        send(
                            moved.at[peer * share + x], gathered.at[slot, x, :, inside],
                            ls.at[k, x], lr.at[k, x], {"vel": peer},
                        )
                    )
        gathered[slot, :, :, at % 256 : at % 256 + wide] = moved[pl.ds(me * share, share)]

    ahead = min(3, chunks)
    for q in range(ahead):
        start_halo(q)

    index = lax.broadcasted_iota(jnp.int32, (1, width), 1) + me * width
    node = lax.broadcasted_iota(jnp.int32, (64, width), 0)
    coef = jnp.ones((64, width), jnp.float32)
    for a in range(3):
        along = lax.shift_right_logical(index, 8 - 4 * a) & 15
        speed = (along.astype(jnp.float32) + 0.5) * (2.0 / VSIDE) - 1.0
        up, down = jnp.maximum(speed, 0.0), jnp.minimum(speed, 0.0)
        line_ref[2 * a : 2 * a + 1, :] = jnp.where(speed > 0, -1.0, 0.0)
        line_ref[2 * a + 1 : 2 * a + 2, :] = jnp.where(speed < 0, 1.0, 0.0)
        line_ref[8 + a : 9 + a, :] = -courant * speed
        digit = lax.shift_right_logical(node, 4 - 2 * a) & 3
        inflow = jnp.where(digit == 3, down, 0.0) - jnp.where(digit == 0, up, 0.0)
        coef = coef + courant * lift_weight * inflow
    coef_ref[...] = coef
    modes = alpha_ref.shape[0]
    for m in range(2 * modes + 1):
        source, row = (alpha_ref, m) if m < modes else (beta_ref, m - modes)
        for i in range(VSIDE):
            kernel_ref[m, i : i + 1, :] = source[row : row + 1, 256 * i : 256 * i + 256]
    loads[chunks].wait()
    lane = lax.broadcasted_iota(jnp.int32, (1, 256), 1)
    shifted = jnp.where(lane >= 160, lane - 160, lane - 64)
    column = lax.shift_right_arithmetic(shifted, 4)

    def weigh(e, carry):
        level = jnp.zeros((1, 256), jnp.int32)
        for face in range(6):
            level = jnp.where(column == face, level_ref[face, e], level)
        total = stack_ref[0] * (level == 0).astype(jnp.float32).astype(low)
        for k in range(1, 5):
            total = total + stack_ref[k] * (level == k).astype(jnp.float32).astype(low)
        w_ref[e] = total
        return carry

    lax.fori_loop(0, elements, weigh, 0, unroll=2)
    loads[chunks + 1].wait()

    for q in range(chunks):
        transport(q)
        if q + ahead < chunks:
            start_halo(q + ahead)

    def returned(k, x, g):
        rows = pl.ds(pl.multiple_of(16 * g, 16), 16)
        return remote(
            mixed.at[peers[k], x, rows], out_ref.at[me * share + x, rows],
            ms.at[k, x, g], mr.at[k, x, g], {"vel": peers[k]},
        )

    def kept(x, g):
        rows = pl.ds(pl.multiple_of(16 * g, 16), 16)
        return pltpu.make_async_copy(
            mixed.at[me, x, rows], out_ref.at[me * share + x, rows], own_sem.at[x, g]
        )

    for copy in moves:
        copy.wait_recv()
    for x in range(share):
        for k in range(ranks - 1):
            lasts[(ranks - 1) * x + k].wait_recv()

        def collide(pair_at, carry):
            both = [2 * pair_at, 2 * pair_at + 1]
            spots = [pl.ds(pl.multiple_of(16 * g, 16), 16) for g in both]
            results = [
                collide_block(
                    gathered[:, x, rows, :].reshape(256, 256), kernel_ref, turn_ref[0],
                    turn_ref[1], turn_ref[2], turn_ref[3],
                )
                for rows in spots
            ]
            for rows, got in zip(spots, results):
                for s in range(ranks):
                    for q in range(groups):
                        at = 16 * (groups * s + q)
                        mixed[s, x, rows, 256 * q : 256 * q + 256] = got[at : at + 16]
            for g in both:
                for k in range(ranks - 1):
                    returned(k, x, g).start()
                kept(x, g).start()
            return carry

        lax.fori_loop(0, 2, collide, 0)

    for copy in halos + moves + lasts:
        copy.wait_send()

    def finish(g, carry):
        for x in range(share):
            for k in range(ranks - 1):
                returned(k, x, g).wait()
            kept(x, g).wait()
        return carry

    lax.fori_loop(0, 4, finish, 0)


def on_device(dist, send_faces, send_count, source_face, subface, alpha, beta):
    low = jnp.bfloat16
    elements, _, vel_local = dist.shape
    slots = send_faces.shape[2]
    ranks = lax.axis_size("vel")
    blocks = lax.axis_size("space")
    spans = [(0, 128), (128, 128)] + [(at, 256) for at in range(256, vel_local, 256)]
    chunks = len(spans)
    share = elements // ranks
    rows = alpha.shape[0] + beta.shape[0]
    smem = pl.BlockSpec(memory_space=pltpu.SMEM)
    vmem = pl.BlockSpec(memory_space=pltpu.VMEM)
    anywhere = pl.BlockSpec(memory_space=pl.ANY)
    hbm = pl.BlockSpec(memory_space=pltpu.HBM)
    stacked, selector = face_parts()
    cosine = cosine_table()
    pair = np.kron(cosine, cosine)
    outer = np.kron(cosine, np.eye(16))
    turns = np.stack([pair.T, pair, outer, outer.T])

    dma = pltpu.SemaphoreType.DMA
    scratch = (
        [pltpu.VMEM((6 * elements + 2 * slots, 16, wide), low) for _, wide in spans]
        + [pltpu.VMEM((2 * slots, 16, wide), low) for _, wide in spans] * 2
        + [pltpu.VMEM((elements, 64, wide), low) for _, wide in spans]
        + [
            pltpu.VMEM((ranks * vel_local // 256, share, 64, 256), low),
            pltpu.VMEM((ranks, share, 64, vel_local), low),
            pltpu.VMEM(dist.shape, low),
            pltpu.VMEM(stacked.shape, low),
            pltpu.VMEM(turns.shape, low),
            pltpu.VMEM((elements, 192, 256), low),
            pltpu.VMEM((64, vel_local), jnp.float32),
            pltpu.VMEM((16, vel_local), jnp.float32),
            pltpu.VMEM((rows, VSIDE, 256), jnp.float32),
        ]
        + [dma((chunks, 2))] * 2
        + [dma((ranks - 1, chunks))] * 2
        + [dma((ranks - 1, share))] * 2
        + [dma((ranks - 1, share, 4))] * 2
        + [dma((share, 4)), dma((chunks + 2,))]
    )
    return pl.pallas_call(
        functools.partial(fused_kernel, (spans, ranks, blocks, slots)),
        out_shape=jax.ShapeDtypeStruct(dist.shape, low),
        in_specs=[smem] * 4 + [hbm, vmem, hbm, vmem, vmem, hbm],
        out_specs=anywhere,
        scratch_shapes=scratch,
        compiler_params=pltpu.CompilerParams(
            collective_id=0, has_side_effects=True, vmem_limit_bytes=56 * 1024 * 1024
        ),
    )(
        send_faces, send_count, source_face.T, subface.T, dist, jnp.asarray(selector, low),
        jnp.asarray(stacked, low), alpha, beta, jnp.asarray(turns, low),
    )


def solution(mesh):
    return jax.shard_map(
        on_device,
        mesh=mesh,
        in_specs=(
            P("space", None, "vel"),
            P("space", None, None),
            P("space", None),
            P("space", None),
            P("space", None),
            P(),
            P(),
        ),
        out_specs=P("space", None, "vel"),
        check_vma=False,
    )
```

```python
import functools

import jax
import jax.numpy as jnp
import numpy as np
from jax import lax
from jax.experimental import pallas as pl
from jax.experimental.pallas import tpu as pltpu
from jax.sharding import PartitionSpec as P

VSIDE = 16
VEL = 4096


courant = 0.1
lift_weight = 6.0
relax_step = 0.5
MESH = pl.DeviceIdType.MESH


def lobatto_points():
    return np.array([-1.0, -1.0 / np.sqrt(5.0), 1.0 / np.sqrt(5.0), 1.0])


def lagrange_table(targets):
    points = lobatto_points()
    result = np.ones((targets.shape[0], 4))
    for column in range(4):
        for second in range(4):
            if second != column:
                result[:, column] = (
                    result[:, column]
                    * (targets - points[second])
                    / (points[column] - points[second])
                )
    return result


def derivative_table():
    points = lobatto_points()
    result = np.zeros((4, 4))
    for row_at in range(4):
        for column in range(4):
            total = 0.0
            for skipped in range(4):
                if skipped != column:
                    factor = 1.0 / (points[column] - points[skipped])
                    for second in range(4):
                        if second != column and second != skipped:
                            factor = (
                                factor
                                * (points[row_at] - points[second])
                                / (points[column] - points[second])
                            )
                    total = total + factor
            result[row_at, column] = total
    return result


def cosine_table():
    index_list = np.arange(VSIDE)
    result = np.sqrt(2.0 / VSIDE) * np.cos(
        np.pi * (index_list[None, :] + 0.5) * index_list[:, None] / VSIDE
    )
    result[0] = result[0] / np.sqrt(2.0)
    return result


def static_tables():
    derivative = derivative_table()
    eye_four = np.eye(4)
    gradients = np.stack(
        [
            np.kron(np.kron(derivative, eye_four), eye_four),
            np.kron(np.kron(eye_four, derivative), eye_four),
            np.kron(np.kron(eye_four, eye_four), derivative),
        ]
    )
    selector = np.zeros((96, 64))
    for axis_at in range(3):
        for side_at in range(2):
            filled = 0
            for node_at in range(64):
                digits = (node_at // 16, node_at // 4 % 4, node_at % 4)
                if digits[axis_at] == 3 * side_at:
                    selector[(2 * axis_at + side_at) * 16 + filled, node_at] = 1.0
                    filled = filled + 1
    points = lobatto_points()
    halves = [lagrange_table((points - 1.0) / 2.0), lagrange_table((points + 1.0) / 2.0)]
    mortar = np.stack(
        [np.eye(16)]
        + [np.kron(halves[(which - 1) // 2], halves[(which - 1) % 2]) for which in range(1, 5)]
    )
    return (gradients, selector, mortar)


def face_parts():
    gradients, selector, mortar = static_tables()
    low = jnp.bfloat16
    grad = np.asarray(gradients.reshape(192, 64).astype(low), np.float64)
    mort = np.asarray(mortar.astype(low), np.float64)
    levels = mort.shape[0]
    spread = np.zeros((levels, 192, 96))
    for face in range(6):
        sel = selector[16 * face : 16 * face + 16]
        for level in range(levels):
            spread[level, 64 * (face // 2) : 64 * (face // 2) + 64, 16 * face : 16 * face + 16] = (
                sel.T @ mort[level]
            )
    stacked = np.concatenate(
        [np.broadcast_to(grad, (levels, 192, 64)), 4.0 * spread, 2.0 * spread], axis=2
    )
    return stacked, selector


def collide_block(values, kernels, pair_t, pair, outer, outer_t):
    low = jnp.bfloat16
    inner = jnp.dot(values, pair_t, preferred_element_type=jnp.float32).astype(low)
    spectrum = jnp.dot(outer, inner, preferred_element_type=jnp.float32).reshape(16, 16, 256)
    rows = kernels.shape[0]
    modes = (rows - 1) // 2

    def field(m):
        scaled = (spectrum * kernels[m][:, None, :]).astype(low).reshape(256, 256)
        back = jnp.dot(scaled, pair, preferred_element_type=jnp.float32).astype(low)
        return jnp.dot(outer_t, back, preferred_element_type=jnp.float32)

    wide = values.astype(jnp.float32)
    total = -wide * field(2 * modes)
    for m in range(modes):
        total = total + field(m) * field(modes + m)
    return (wide + relax_step * total).astype(low)


def fused_kernel(
    sizes, send_ref, count_ref, source_ref, level_ref, dist_hbm, select_ref, stack_hbm, alpha_ref,
    beta_ref, tables_hbm, out_ref, *scratch,
):
    spans, ranks, blocks, slots = sizes
    chunks = len(spans)
    tables, halo_out, halo_in, moved_out = (
        scratch[chunks * k : chunks * k + chunks] for k in range(4)
    )
    rest = scratch[4 * chunks :]
    gathered, mixed, dist_ref, stack_ref, turn_ref = rest[:5]
    w_ref, coef_ref, line_ref, kernel_ref = rest[5:9]
    hs, hr, us, ur, ls, lr, ms, mr, own_sem, in_sem = rest[9:]
    elements, _, width = dist_ref.shape
    share = elements // ranks
    groups = width // 256
    local = 6 * elements
    low = jnp.bfloat16
    place = lax.axis_index("space")
    me = lax.axis_index("vel")
    after = lax.rem(place + 1, blocks)
    before = lax.rem(place + blocks - 1, blocks)
    far_first = sorted(range(1, ranks), key=lambda k: abs(2 * k - ranks))
    peers = [lax.rem(me + k, ranks) for k in far_first]

    barrier = pltpu.get_barrier_semaphore()
    for other in (before, after):
        pl.semaphore_signal(barrier, inc=1, device_id={"space": other}, device_id_type=MESH)
    for peer in peers:
        pl.semaphore_signal(barrier, inc=1, device_id={"vel": peer}, device_id_type=MESH)

    loads = [
        pltpu.make_async_copy(
            dist_hbm.at[:, :, pl.ds(at, wide)], dist_ref.at[:, :, pl.ds(at, wide)], in_sem.at[q]
        )
        for q, (at, wide) in enumerate(spans)
    ]
    loads.append(pltpu.make_async_copy(stack_hbm, stack_ref, in_sem.at[chunks]))
    loads.append(pltpu.make_async_copy(tables_hbm, turn_ref, in_sem.at[chunks + 1]))
    for copy in loads:
        copy.start()

    def remote(src, dst, send_sem, recv_sem, target):
        return pltpu.make_async_remote_copy(
            src_ref=src, dst_ref=dst, send_sem=send_sem, recv_sem=recv_sem,
            device_id=target, device_id_type=MESH,
        )

    def send(*args):
        copy = remote(*args)
        copy.start()
        return copy

    halos, moves, lasts = [], [], []

    def start_halo(q):
        at, wide = spans[q]
        lanes = slice(at, at + wide)
        table, outgoing = tables[q], halo_out[q]
        loads[q].wait()

        def fill(e, carry):
            got = jnp.dot(select_ref[...], dist_ref[e, :, lanes], preferred_element_type=jnp.float32)
            table[pl.ds(6 * e, 6)] = got.astype(low).reshape(6, 16, wide)
            return carry

        lax.fori_loop(0, elements, fill, 0, unroll=4)
        for j in range(2):

            def pick(m, carry):
                live = (m < count_ref[0, j]).astype(low)
                outgoing[slots * j + m] = table[send_ref[0, j, m]] * live
                return carry

            lax.fori_loop(0, slots, pick, 0, unroll=4)
        if q == 0:
            pl.semaphore_wait(barrier, ranks + 1)
        for j, target in ((1, after), (0, before)):
            halos.append(
                send(
                    outgoing.at[pl.ds(slots * j, slots)],
                    halo_in[q].at[pl.ds(slots * (1 - j), slots)],
                    hs.at[q, j], hr.at[q, j], {"space": target},
                )
            )

    def transport(q):
        at, wide = spans[q]
        lanes = slice(at, at + wide)
        table, moved = tables[q], moved_out[q]
        halos[2 * q].wait_recv()
        halos[2 * q + 1].wait_recv()
        table[local : local + 2 * slots] = halo_in[q][...]
        signs = [line_ref[face : face + 1, lanes].astype(low) for face in range(6)]

        def step(e, carry):
            here = dist_ref[e, :, lanes]
            near = [table[source_ref[face, e]] * signs[face] for face in range(6)]
            stacked = jnp.concatenate([here] + near + near, axis=0)
            parts = jnp.dot(w_ref[e], stacked, preferred_element_type=jnp.float32)
            total = coef_ref[:, lanes] * here.astype(jnp.float32)
            for a in range(3):
                total = total + line_ref[8 + a : 9 + a, lanes] * parts[64 * a : 64 * a + 64]
            moved[e] = total.astype(low)
            return carry

        lax.fori_loop(0, elements, step, 0, unroll=2)
        slot = me * groups + at // 256
        inside = pl.ds(at % 256, wide)
        if q < chunks - 1:
            for k, peer in enumerate(peers):
                moves.append(
                    send(
                        moved.at[pl.ds(peer * share, share)], gathered.at[slot, :, :, inside],
                        us.at[k, q], ur.at[k, q], {"vel": peer},
                    )
                )
        else:
            for x in range(share):
                for k, peer in enumerate(peers):
                    lasts.append(
                        send(
                            moved.at[peer * share + x], gathered.at[slot, x, :, inside],
                            ls.at[k, x], lr.at[k, x], {"vel": peer},
                        )
                    )
        gathered[slot, :, :, at % 256 : at % 256 + wide] = moved[pl.ds(me * share, share)]

    ahead = min(3, chunks)
    for q in range(ahead):
        start_halo(q)

    index = lax.broadcasted_iota(jnp.int32, (1, width), 1) + me * width
    node = lax.broadcasted_iota(jnp.int32, (64, width), 0)
    coef = jnp.ones((64, width), jnp.float32)
    for a in range(3):
        along = lax.shift_right_logical(index, 8 - 4 * a) & 15
        speed = (along.astype(jnp.float32) + 0.5) * (2.0 / VSIDE) - 1.0
        up, down = jnp.maximum(speed, 0.0), jnp.minimum(speed, 0.0)
        line_ref[2 * a : 2 * a + 1, :] = jnp.where(speed > 0, -1.0, 0.0)
        line_ref[2 * a + 1 : 2 * a + 2, :] = jnp.where(speed < 0, 1.0, 0.0)
        line_ref[8 + a : 9 + a, :] = -courant * speed
        digit = lax.shift_right_logical(node, 4 - 2 * a) & 3
        inflow = jnp.where(digit == 3, down, 0.0) - jnp.where(digit == 0, up, 0.0)
        coef = coef + courant * lift_weight * inflow
    coef_ref[...] = coef
    modes = alpha_ref.shape[0]
    for m in range(2 * modes + 1):
        source, row = (alpha_ref, m) if m < modes else (beta_ref, m - modes)
        for i in range(VSIDE):
            kernel_ref[m, i : i + 1, :] = source[row : row + 1, 256 * i : 256 * i + 256]
    loads[chunks].wait()
    lane = lax.broadcasted_iota(jnp.int32, (1, 256), 1)
    shifted = jnp.where(lane >= 160, lane - 160, lane - 64)
    column = lax.shift_right_arithmetic(shifted, 4)

    def weigh(e, carry):
        level = jnp.zeros((1, 256), jnp.int32)
        for face in range(6):
            level = jnp.where(column == face, level_ref[face, e], level)
        total = stack_ref[0] * (level == 0).astype(jnp.float32).astype(low)
        for k in range(1, 5):
            total = total + stack_ref[k] * (level == k).astype(jnp.float32).astype(low)
        w_ref[e] = total
        return carry

    lax.fori_loop(0, elements, weigh, 0, unroll=2)
    loads[chunks + 1].wait()

    for q in range(chunks):
        transport(q)
        if q + ahead < chunks:
            start_halo(q + ahead)

    def returned(k, x, g):
        rows = pl.ds(pl.multiple_of(16 * g, 16), 16)
        return remote(
            mixed.at[peers[k], x, rows], out_ref.at[me * share + x, rows],
            ms.at[k, x, g], mr.at[k, x, g], {"vel": peers[k]},
        )

    def kept(x, g):
        rows = pl.ds(pl.multiple_of(16 * g, 16), 16)
        return pltpu.make_async_copy(
            mixed.at[me, x, rows], out_ref.at[me * share + x, rows], own_sem.at[x, g]
        )

    for copy in moves:
        copy.wait_recv()
    for x in range(share):
        for k in range(ranks - 1):
            lasts[(ranks - 1) * x + k].wait_recv()

        def collide(g, carry):
            rows = pl.ds(pl.multiple_of(16 * g, 16), 16)
            values = gathered[:, x, rows, :].reshape(256, 256)
            got = collide_block(
                values, kernel_ref, turn_ref[0], turn_ref[1], turn_ref[2], turn_ref[3]
            )
            for s in range(ranks):
                for q in range(groups):
                    at = 16 * (groups * s + q)
                    mixed[s, x, rows, 256 * q : 256 * q + 256] = got[at : at + 16]
            for k in range(ranks - 1):
                returned(k, x, g).start()
            kept(x, g).start()
            return carry

        lax.fori_loop(0, 4, collide, 0)

    for copy in halos + moves + lasts:
        copy.wait_send()

    def finish(g, carry):
        for x in range(share):
            for k in range(ranks - 1):
                returned(k, x, g).wait()
            kept(x, g).wait()
        return carry

    lax.fori_loop(0, 4, finish, 0)


def on_device(dist, send_faces, send_count, source_face, subface, alpha, beta):
    low = jnp.bfloat16
    elements, _, vel_local = dist.shape
    slots = send_faces.shape[2]
    ranks = lax.axis_size("vel")
    blocks = lax.axis_size("space")
    spans = [(0, 128), (128, 128)] + [(at, 256) for at in range(256, vel_local, 256)]
    if vel_local > 256:
        spans[-1:] = [(vel_local - 256, 128), (vel_local - 128, 128)]
    chunks = len(spans)
    share = elements // ranks
    rows = alpha.shape[0] + beta.shape[0]
    smem = pl.BlockSpec(memory_space=pltpu.SMEM)
    vmem = pl.BlockSpec(memory_space=pltpu.VMEM)
    anywhere = pl.BlockSpec(memory_space=pl.ANY)
    hbm = pl.BlockSpec(memory_space=pltpu.HBM)
    stacked, selector = face_parts()
    cosine = cosine_table()
    pair = np.kron(cosine, cosine)
    outer = np.kron(cosine, np.eye(16))
    turns = np.stack([pair.T, pair, outer, outer.T])

    dma = pltpu.SemaphoreType.DMA
    scratch = (
        [pltpu.VMEM((6 * elements + 2 * slots, 16, wide), low) for _, wide in spans]
        + [pltpu.VMEM((2 * slots, 16, wide), low) for _, wide in spans] * 2
        + [pltpu.VMEM((elements, 64, wide), low) for _, wide in spans]
        + [
            pltpu.VMEM((ranks * vel_local // 256, share, 64, 256), low),
            pltpu.VMEM((ranks, share, 64, vel_local), low),
            pltpu.VMEM(dist.shape, low),
            pltpu.VMEM(stacked.shape, low),
            pltpu.VMEM(turns.shape, low),
            pltpu.VMEM((elements, 192, 256), low),
            pltpu.VMEM((64, vel_local), jnp.float32),
            pltpu.VMEM((16, vel_local), jnp.float32),
            pltpu.VMEM((rows, VSIDE, 256), jnp.float32),
        ]
        + [dma((chunks, 2))] * 2
        + [dma((ranks - 1, chunks))] * 2
        + [dma((ranks - 1, share))] * 2
        + [dma((ranks - 1, share, 4))] * 2
        + [dma((share, 4)), dma((chunks + 2,))]
    )
    return pl.pallas_call(
        functools.partial(fused_kernel, (spans, ranks, blocks, slots)),
        out_shape=jax.ShapeDtypeStruct(dist.shape, low),
        in_specs=[smem] * 4 + [hbm, vmem, hbm, vmem, vmem, hbm],
        out_specs=anywhere,
        scratch_shapes=scratch,
        compiler_params=pltpu.CompilerParams(
            collective_id=0, has_side_effects=True, vmem_limit_bytes=56 * 1024 * 1024
        ),
    )(
        send_faces, send_count, source_face.T, subface.T, dist, jnp.asarray(selector, low),
        jnp.asarray(stacked, low), alpha, beta, jnp.asarray(turns, low),
    )


def solution(mesh):
    return jax.shard_map(
        on_device,
        mesh=mesh,
        in_specs=(
            P("space", None, "vel"),
            P("space", None, None),
            P("space", None),
            P("space", None),
            P("space", None),
            P(),
            P(),
        ),
        out_specs=P("space", None, "vel"),
        check_vma=False,
    )
```
